256 devices in a mesh: seq: 32 (over z, y), win: 8 (over x, core).
Axes of the slice: x: 4, y: 4, z: 8, core: 2. Of those that a mesh axis runs over, the one named last changes fastest.
Arguments:
- bases: int32 [8, 8192], P('win', 'seq'), may hold values from 0 to 3
- stem_weight: float32 [20, 768], replicated, may hold values from -3 to 3
- norm_gain: float32 [768], replicated, may hold values from 0.1 to 1.9
- conv_weight: bfloat16 [3840, 768], P(('seq', 'win')), may hold values from -0.09375 to 0.09375
- cotangent: bfloat16 [8, 4096, 768], P('win', 'seq'), may hold values from -0.079589844 to 0.079589844
Outputs:
- conv_grad: float32 [3840, 768], P(('seq', 'win'))
- stem_grad: float32 [20, 768], replicated
- gain_grad: float32 [768], replicated
The draws below stay inside these ranges and needn't reach their ends.
All inputs are finite; a program needn't handle non-finite values.
Results may differ from the reference program's by a relative error of at most 0.0044.
Values may be sent and summed in bfloat16 or wider, within the bound.
No kernel may reach another device: no remote copies, remote signals or barrier semaphores. Data moves between devices by JAX's collectives and lax.ppermute only.
A program may use at most 64 MiB of HBM per device.

```python
import jax
import jax.numpy as jnp
from jax import lax

C = 768
KW = 5
WIN = 8
L = 8192
HALF = 4096


def with_ends(drawn, rng, smallest, largest):
    shape = drawn.shape
    spot = [jax.random.randint(jax.random.fold_in(rng, axis), (), 0, shape[axis]) for axis in range(len(shape))]
    drawn = drawn.at[tuple(spot)].set(smallest)
    longest = shape.index(max(shape))
    spot[longest] = (spot[longest] + 1) % shape[longest]
    return drawn.at[tuple(spot)].set(largest)


def level_of(key, dims, cuts, smallest, high):
    loudness, own = 1.0, jax.random.fold_in(key, 6)
    for dim, blocks in cuts:
        steps = jnp.exp(jax.random.uniform(jax.random.fold_in(own, dim), (blocks,), jnp.float32, smallest / len(cuts), high / len(cuts)))
        loudness = loudness * jnp.repeat(steps, dims[dim] // blocks).reshape([-1 if axis == dim else 1 for axis in range(len(dims))])
    return loudness


def scatter_about(rng, dims, spread, bound, shards=(), held_as=jnp.bfloat16):
    array = jax.random.normal(rng, dims, jnp.float32) * spread
    if len(shards) > 0:
        array = level_of(rng, dims, shards, -0.22, 0.18) * array
    return jnp.clip(array, min=-bound, max=bound).astype(held_as)


def setup_inputs(seed: int = 0) -> dict:
    key_list = jax.random.split(jax.random.key(seed), 6)
    return {
        "bases": with_ends(jax.random.randint(key_list[0], (WIN, L), 0, 4), jax.random.fold_in(key_list[0], 1), 0, 3).astype(jnp.int32),
        "stem_weight": scatter_about(key_list[1], (4 * KW, C), 0.5, 3.0, (), jnp.float32),
        "norm_gain": jnp.clip(1.0 + 0.18 * jax.random.normal(key_list[2], (C,), jnp.float32), 0.1, 1.9),
        "conv_weight": scatter_about(key_list[3], (KW * C, C), (KW * C) ** -0.5, 0.09375, ((0, 256),)),
        "cotangent": scatter_about(key_list[4], (WIN, HALF, C), 0.01, 0.079589844, ((0, 8), (1, 32))),
    }


def norm_rows(x0, gain):
    scale = lax.rsqrt(lax.optimization_barrier(jnp.mean(x0 * x0, axis=-1, keepdims=True)) + 1e-06)
    return x0 * scale * gain

def gelu_back(pre, upstream):
    return jax.vjp(jax.nn.gelu, pre)[1](upstream)[0]

def one_window(bases_row, cot_row, stem_weight, norm_gain, conv_weight):
    length = bases_row.shape[0]
    channels = norm_gain.shape[0]
    onehot = (bases_row[:, None] == jnp.arange(4, dtype=jnp.int32)[None, :]).astype(jnp.float32)
    padded = jnp.pad(onehot, ((2, 2), (0, 0)))
    stem_cols = jnp.concatenate([padded[t:t + length] for t in range(KW)], axis=1)
    x0 = jnp.dot(stem_cols, stem_weight, precision=lax.Precision.HIGHEST, preferred_element_type=jnp.float32)
    xn = norm_rows(x0, norm_gain).astype(jnp.bfloat16)
    xpad = jnp.pad(xn, ((2, 2), (0, 0)))
    conv_cols = jnp.concatenate([xpad[t:t + length] for t in range(KW)], axis=1)
    pre = jnp.dot(conv_cols, conv_weight, preferred_element_type=jnp.float32)
    upstream = 0.5 * jnp.repeat(cot_row.astype(jnp.float32), 2, axis=0)
    dpre = gelu_back(pre, upstream).astype(jnp.bfloat16)
    conv_part = jnp.dot(conv_cols.T, dpre, preferred_element_type=jnp.float32)
    dpad = jnp.pad(dpre, ((2, 2), (0, 0)))
    dxn = jnp.zeros((length, channels), jnp.float32)
    for t in range(KW):
        dxn = dxn + jnp.dot(dpad[4 - t:4 - t + length], conv_weight[t * channels:(t + 1) * channels].T, preferred_element_type=jnp.float32)
    back = jax.vjp(norm_rows, x0, norm_gain)[1](dxn)
    dx0 = upstream + back[0]
    stem_part = jnp.dot(stem_cols.T, dx0, precision=lax.Precision.HIGHEST, preferred_element_type=jnp.float32)
    return (conv_part, stem_part, back[1])

def reference(bases, stem_weight, norm_gain, conv_weight, cotangent):

    def step(carry, items):
        parts = one_window(items[0], items[1], stem_weight, norm_gain, conv_weight)
        return ((carry[0] + parts[0], carry[1] + parts[1], carry[2] + parts[2]), None)
    init = (jnp.zeros(conv_weight.shape, jnp.float32), jnp.zeros(stem_weight.shape, jnp.float32), jnp.zeros(norm_gain.shape, jnp.float32))
    totals, unused = lax.scan(step, init, (bases, cotangent))
    return (totals[0], totals[1], totals[2])
```

```python
import functools

import jax
import jax.numpy as jnp
from jax import lax
from jax.experimental import pallas as pl
from jax.experimental.pallas import tpu as pltpu
from jax.sharding import PartitionSpec as P

KW = 5
AXES = ("seq", "win")
F32 = jnp.float32
BF16 = jnp.bfloat16
HIGH = lax.Precision.HIGHEST
ROOT = 0.7978845608028654
CUBE = 0.044715


def pieces(x, count):
    out = []
    for _ in range(count):
        top = x.astype(BF16)
        out.append(top)
        x = x - top.astype(F32)
    return out


def gelu_slope(x):
    sq = x * x
    th = jnp.tanh(ROOT * x * (1.0 + CUBE * sq))
    return 0.5 * (1.0 + th) + (0.5 * ROOT) * x * (1.0 - th * th) * (1.0 + 3.0 * CUBE * sq)


def main_kernel(channels, sym_ref, dr_ref, table_ref, out_ref):
    lanes = dr_ref.shape[-1]
    lane = lax.broadcasted_iota(jnp.int32, (8, lanes), 1)
    sub = lax.broadcasted_iota(jnp.int32, (8, lanes), 0)
    top = sub < 4
    first, last = lane == 0, lane == lanes - 1
    base = (sub % 4).astype(F32)

    def down(x, fill):
        return jnp.where(first, fill, pltpu.roll(x, 1, 1))

    def up(x, fill):
        return jnp.where(last, fill, pltpu.roll(x, lanes - 1, 1))

    table = table_ref[...]

    def window(w, total):
        sym = sym_ref[w]
        mid = jnp.where(top, sym[0:1], sym[1:2])
        hot = [
            (cell == base).astype(F32) for cell in (down(mid, -1.0), mid, up(mid, -1.0))
        ]
        hots = jnp.concatenate(hot, axis=0)
        narrow = hots.astype(BF16)
        looked = jnp.dot(
            table, jnp.concatenate([narrow] * 3, axis=0), preferred_element_type=F32
        )
        taps = [looked[8 * t : 8 * t + 8] for t in range(KW)]
        mean_e = jnp.sum(looked[40:64] * hots, axis=0, keepdims=True)
        mean_o = jnp.sum(looked[64:88] * hots, axis=0, keepdims=True)
        scale_e = lax.rsqrt(mean_e + 1e-06)
        scale_o = lax.rsqrt(mean_o + 1e-06)
        scale = jnp.where(top, scale_e, scale_o)
        swapped = jnp.where(top, scale_o, scale_e)
        p0, p2, p4 = taps[0] * scale, taps[2] * scale, taps[4] * scale
        p1, p3 = taps[1] * swapped, taps[3] * swapped
        pre = down(p0 + jnp.where(top, p1, 0.0), 0.0)
        pre = pre + p2 + jnp.where(top, p3, p1)
        pre = pre + up(p4 + jnp.where(top, 0.0, p3), 0.0)
        dr = dr_ref[w].astype(F32)
        dpre = dr * gelu_slope(pre)
        ahead, behind = up(dpre, 0.0), down(dpre, 0.0)
        d1 = jnp.where(top, ahead, dpre)
        d3 = jnp.where(top, dpre, behind)
        here = taps[0] * ahead + taps[2] * dpre + taps[4] * behind
        there = taps[1] * d1 + taps[3] * d3
        both = here + pltpu.roll(there, 4, 0)
        q_e = jnp.sum(jnp.where(top, both, 0.0), axis=0, keepdims=True)
        q_o = jnp.sum(jnp.where(top, 0.0, both), axis=0, keepdims=True)
        u_e = q_e * scale_e * scale_e * scale_e * (1.0 / channels)
        u_o = q_o * scale_o * scale_o * scale_o * (1.0 / channels)
        rows = [ahead * scale, d1 * swapped, dpre * scale, d3 * swapped, behind * scale, dr]
        rows = jnp.concatenate(rows + [hots * u_e, hots * u_o], axis=0)
        found = jnp.zeros((rows.shape[0], 24), F32)
        for part in pieces(rows, 2):
            found = found + lax.dot_general(
                part, narrow, (((1,), (1,)), ((), ())), preferred_element_type=F32
            )
        return total + found

    out_ref[...] = lax.fori_loop(
        0, sym_ref.shape[0], window, jnp.zeros(out_ref.shape, F32)
    )


def main_call(channels, sym, dr, table):
    return pl.pallas_call(
        functools.partial(main_kernel, channels),
        out_shape=jax.ShapeDtypeStruct((96, 24), F32),
        in_specs=[pl.BlockSpec(memory_space=pltpu.VMEM)] * 3,
        out_specs=pl.BlockSpec(memory_space=pltpu.VMEM),
        compiler_params=pltpu.CompilerParams(vmem_limit_bytes=40 * 1024 * 1024),
    )(sym, dr, table)


def exchange(x):
    return lax.all_to_all(x, AXES, 0, 0, tiled=True)


def shards(bases, stem_weight, norm_gain, conv_weight, cotangent):
    seq, win = lax.axis_size("seq"), lax.axis_size("win")
    n = seq * win
    channels = norm_gain.shape[0]
    cols = channels // n
    half = bases.shape[1] // 2
    share = conv_weight.shape[0]
    taps = 4 * KW

    cot = cotangent[0].reshape(half, cols, n).transpose(2, 1, 0)
    own = conv_weight.reshape(share, cols, n).transpose(2, 1, 0)
    even_odd = bases[0].reshape(half, 2).T.astype(BF16)
    sent = jnp.concatenate(
        [
            cot.reshape(n, cols * half),
            jnp.broadcast_to(even_odd.reshape(1, 2 * half), (n, 2 * half)),
            own.reshape(n, cols * share),
        ],
        axis=1,
    )
    got = exchange(sent)
    cot = got[:, : cols * half].reshape(seq, win, cols, half).transpose(1, 2, 0, 3)
    cot = cot.reshape(win, cols, seq * half)
    dr = jnp.pad(0.5 * cot, ((0, 0), (0, 4 - cols), (0, 0)))
    dr = jnp.concatenate([dr, dr], axis=1)
    sym = got[:, cols * half : (cols + 2) * half].reshape(seq, win, 2, half)
    sym = sym.transpose(1, 2, 0, 3).reshape(win, 2, seq * half).astype(F32)
    weights = got[:, (cols + 2) * half :].reshape(n, cols, share)
    weights = weights.transpose(1, 0, 2).reshape(cols, KW, channels).astype(F32)

    gained = stem_weight * norm_gain
    mixed = jnp.einsum("kc,mtc->tmk", gained, weights, precision=HIGH)
    gram = jnp.dot(stem_weight, stem_weight.T, precision=HIGH) * (1.0 / channels)
    even = jnp.pad(mixed, ((0, 0), (0, 4 - cols), (0, 4)))
    odd = jnp.pad(mixed, ((0, 0), (0, 4 - cols), (4, 0)))
    swap = (jnp.arange(KW) % 2 == 1)[:, None, None]
    table = jnp.concatenate(
        [jnp.where(swap, odd, even), jnp.where(swap, even, odd)], axis=1
    ).reshape(8 * KW, 24)
    table = jnp.concatenate(
        [table, jnp.pad(gram, ((0, 4), (0, 4))), jnp.pad(gram, ((4, 0), (4, 0)))], axis=0
    )
    table = jnp.concatenate(pieces(table, 3), axis=1)

    found = main_call(channels, sym, dr, table)

    sums = found[:48].reshape(6, 2, 4, 24)[:, :, :cols]
    swap = jnp.concatenate([swap, swap[:1]], axis=0)
    sums = jnp.where(
        swap,
        sums[:, 0, :, 4:] + sums[:, 1, :, :taps],
        sums[:, 0, :, :taps] + sums[:, 1, :, 4:],
    )
    grads, direct = sums[:KW], sums[KW]
    crossed = found[48 : 48 + taps, :taps] + found[76:96, 4:]
    conv_rows = jnp.einsum("tmk,kc->mtc", grads, gained, precision=HIGH)
    conv_rows = conv_rows.reshape(cols, n, share).transpose(1, 2, 0).reshape(n, share * cols)
    back = jnp.einsum("tmk,mtc->kc", grads, weights, precision=HIGH)
    stem_part = norm_gain * back - jnp.dot(crossed, stem_weight, precision=HIGH)
    gain_part = jnp.sum(stem_weight * back, axis=0, keepdims=True)
    small = jnp.concatenate([stem_part, gain_part], axis=0)
    small = small.reshape(taps + 1, cols, n).transpose(2, 0, 1).reshape(n, (taps + 1) * cols)
    got = exchange(jnp.concatenate([conv_rows, small], axis=1))
    conv_grad = got[:, : share * cols].T.reshape(share, channels)
    mine = jnp.sum(got[:, share * cols :], axis=0)
    mine = mine + jnp.pad(direct.T, ((0, 1), (0, 0))).reshape(-1)
    full = exchange(jnp.broadcast_to(mine[None], (n, mine.shape[0])))
    full = full.T.reshape(taps + 1, channels)
    return (conv_grad, full[:taps], full[taps])


def solution(mesh):
    in_specs = (P("win", "seq"), P(), P(), P(("seq", "win"), None), P("win", "seq", None))
    out_specs = (P(("seq", "win"), None), P(), P())
    return jax.shard_map(shards, mesh=mesh, in_specs=in_specs, out_specs=out_specs, check_vma=False)
```

```python
import functools

import jax
import jax.numpy as jnp
from jax import lax
from jax.experimental import pallas as pl
from jax.experimental.pallas import tpu as pltpu
from jax.sharding import PartitionSpec as P

KW = 5
AXES = ("seq", "win")
F32 = jnp.float32
BF16 = jnp.bfloat16
HIGH = lax.Precision.HIGHEST
ROOT = 0.7978845608028654
CUBE = 0.044715


def pieces(x, count):
    out = []
    for _ in range(count):
        top = x.astype(BF16)
        out.append(top)
        x = x - top.astype(F32)
    return out


def gelu_slope(x):
    sq = x * x
    th = jnp.tanh(ROOT * x * (1.0 + CUBE * sq))
    return 0.5 * (1.0 + th) + (0.5 * ROOT) * x * (1.0 - th * th) * (1.0 + 3.0 * CUBE * sq)


def main_kernel(channels, sym_ref, dr_ref, table_ref, out_ref):
    lanes = dr_ref.shape[-1]
    lane = lax.broadcasted_iota(jnp.int32, (8, lanes), 1)
    sub = lax.broadcasted_iota(jnp.int32, (8, lanes), 0)
    top = sub < 4
    first, last = lane == 0, lane == lanes - 1
    base = (sub % 4).astype(F32)

    def down(x, fill):
        return jnp.where(first, fill, pltpu.roll(x, 1, 1))

    def up(x, fill):
        return jnp.where(last, fill, pltpu.roll(x, lanes - 1, 1))

    table = table_ref[...]

    def window(w, total):
        sym = sym_ref[w]
        mid = jnp.where(top, sym[0:1], sym[1:2])
        hot = [
            (cell == base).astype(F32) for cell in (down(mid, -1.0), mid, up(mid, -1.0))
        ]
        hots = jnp.concatenate(hot, axis=0)
        narrow = hots.astype(BF16)
        looked = jnp.dot(
            table, jnp.concatenate([narrow] * 3, axis=0), preferred_element_type=F32
        )
        taps = [looked[8 * t : 8 * t + 8] for t in range(KW)]
        mean_e = jnp.sum(looked[40:64] * hots, axis=0, keepdims=True)
        mean_o = jnp.sum(looked[64:88] * hots, axis=0, keepdims=True)
        scale_e = lax.rsqrt(mean_e + 1e-06)
        scale_o = lax.rsqrt(mean_o + 1e-06)
        scale = jnp.where(top, scale_e, scale_o)
        swapped = jnp.where(top, scale_o, scale_e)
        p0, p2, p4 = taps[0] * scale, taps[2] * scale, taps[4] * scale
        p1, p3 = taps[1] * swapped, taps[3] * swapped
        pre = down(p0 + jnp.where(top, p1, 0.0), 0.0)
        pre = pre + p2 + jnp.where(top, p3, p1)
        pre = pre + up(p4 + jnp.where(top, 0.0, p3), 0.0)
        dr = dr_ref[w].astype(F32)
        dpre = dr * gelu_slope(pre)
        ahead, behind = up(dpre, 0.0), down(dpre, 0.0)
        d1 = jnp.where(top, ahead, dpre)
        d3 = jnp.where(top, dpre, behind)
        here = taps[0] * ahead + taps[2] * dpre + taps[4] * behind
        there = taps[1] * d1 + taps[3] * d3
        both = here + pltpu.roll(there, 4, 0)
        q_e = jnp.sum(jnp.where(top, both, 0.0), axis=0, keepdims=True)
        q_o = jnp.sum(jnp.where(top, 0.0, both), axis=0, keepdims=True)
        u_e = q_e * scale_e * scale_e * scale_e * (1.0 / channels)
        u_o = q_o * scale_o * scale_o * scale_o * (1.0 / channels)
        rows = [ahead * scale, d1 * swapped, dpre * scale, d3 * swapped, behind * scale, dr]
        rows = jnp.concatenate(rows + [hots * u_e, hots * u_o], axis=0)
        found = lax.dot_general(
            rows.astype(BF16), narrow, (((1,), (1,)), ((), ())), preferred_element_type=F32
        )
        return total + found

    total = jnp.zeros(out_ref.shape, F32)
    for w in range(sym_ref.shape[0]):
        total = window(w, total)
    out_ref[...] = total


def main_call(channels, sym, dr, table):
    return pl.pallas_call(
        functools.partial(main_kernel, channels),
        out_shape=jax.ShapeDtypeStruct((96, 24), F32),
        in_specs=[pl.BlockSpec(memory_space=pltpu.VMEM)] * 3,
        out_specs=pl.BlockSpec(memory_space=pltpu.VMEM),
        compiler_params=pltpu.CompilerParams(vmem_limit_bytes=40 * 1024 * 1024),
    )(sym, dr, table)


def exchange(x):
    return lax.all_to_all(x, AXES, 0, 0, tiled=True)


def shards(bases, stem_weight, norm_gain, conv_weight, cotangent):
    seq, win = lax.axis_size("seq"), lax.axis_size("win")
    n = seq * win
    channels = norm_gain.shape[0]
    cols = channels // n
    half = bases.shape[1] // 2
    share = conv_weight.shape[0]
    taps = 4 * KW

    cot = cotangent[0].reshape(half, cols, n).transpose(2, 1, 0)
    own = conv_weight.reshape(share, cols, n).transpose(2, 1, 0)
    even_odd = bases[0].reshape(half, 2).T.astype(BF16).reshape(1, 2 * half)
    second = jnp.concatenate(
        [
            jnp.broadcast_to(even_odd, (n, 2 * half)),
            own.reshape(n, cols * share),
            jnp.zeros((n, (cols - 2) * half - cols * share), BF16),
        ],
        axis=1,
    )
    sent = jnp.stack([cot.reshape(n, cols * half), second], axis=1)
    got = exchange(sent)
    cot = got[:, 0].reshape(seq, win, cols, half).transpose(1, 2, 0, 3)
    cot = cot.reshape(win, cols, seq * half)
    dr = jnp.pad(0.5 * cot, ((0, 0), (0, 4 - cols), (0, 0)))
    dr = jnp.concatenate([dr, dr], axis=1)
    sym = got[:, 1, : 2 * half].reshape(seq, win, 2, half)
    sym = sym.transpose(1, 2, 0, 3).reshape(win, 2, seq * half).astype(F32)
    weights = got[:, 1, 2 * half : 2 * half + cols * share].reshape(n, cols, share)
    weights = weights.transpose(1, 0, 2).reshape(cols, KW, channels).astype(F32)

    gained = stem_weight * norm_gain
    mixed = jnp.einsum("kc,mtc->tmk", gained, weights, precision=HIGH)
    gram = jnp.dot(stem_weight, stem_weight.T, precision=HIGH) * (1.0 / channels)
    even = jnp.pad(mixed, ((0, 0), (0, 4 - cols), (0, 4)))
    odd = jnp.pad(mixed, ((0, 0), (0, 4 - cols), (4, 0)))
    swap = (jnp.arange(KW) % 2 == 1)[:, None, None]
    table = jnp.concatenate(
        [jnp.where(swap, odd, even), jnp.where(swap, even, odd)], axis=1
    ).reshape(8 * KW, 24)
    table = jnp.concatenate(
        [table, jnp.pad(gram, ((0, 4), (0, 4))), jnp.pad(gram, ((4, 0), (4, 0)))], axis=0
    )
    table = jnp.concatenate(pieces(table, 3), axis=1)

    found = main_call(channels, sym, dr, table)

    sums = found[:48].reshape(6, 2, 4, 24)[:, :, :cols]
    swap = jnp.concatenate([swap, swap[:1]], axis=0)
    sums = jnp.where(
        swap,
        sums[:, 0, :, 4:] + sums[:, 1, :, :taps],
        sums[:, 0, :, :taps] + sums[:, 1, :, 4:],
    )
    grads, direct = sums[:KW], sums[KW]
    crossed = found[48 : 48 + taps, :taps] + found[76:96, 4:]
    conv_rows = jnp.einsum("tmk,kc->mtc", grads, gained, precision=HIGH)
    conv_rows = conv_rows.reshape(cols, n, share).transpose(1, 2, 0).reshape(n, share * cols)
    back = jnp.einsum("tmk,mtc->kc", grads, weights, precision=HIGH)
    stem_part = norm_gain * back - jnp.dot(crossed, stem_weight, precision=HIGH)
    gain_part = jnp.sum(stem_weight * back, axis=0, keepdims=True)
    small = jnp.concatenate([stem_part, gain_part], axis=0)
    small = small.reshape(taps + 1, cols, n).transpose(2, 0, 1).reshape(n, (taps + 1) * cols)
    got = exchange(jnp.concatenate([conv_rows, small], axis=1))
    conv_grad = got[:, : share * cols].T.reshape(share, channels)
    mine = jnp.sum(got[:, share * cols :], axis=0)
    mine = mine + jnp.pad(direct.T, ((0, 1), (0, 0))).reshape(-1)
    full = exchange(jnp.broadcast_to(mine[None], (n, mine.shape[0])))
    full = full.T.reshape(taps + 1, channels)
    return (conv_grad, full[:taps], full[taps])


def solution(mesh):
    in_specs = (P("win", "seq"), P(), P(), P(("seq", "win"), None), P("win", "seq", None))
    out_specs = (P(("seq", "win"), None), P(), P())
    return jax.shard_map(shards, mesh=mesh, in_specs=in_specs, out_specs=out_specs, check_vma=False)
```

```python
import functools

import jax
import jax.numpy as jnp
from jax import lax
from jax.experimental import pallas as pl
from jax.experimental.pallas import tpu as pltpu
from jax.sharding import PartitionSpec as P

KW = 5
TAPS = 4 * KW
AXES = ("seq", "win")
F32 = jnp.float32
BF16 = jnp.bfloat16
HIGH = lax.Precision.HIGHEST
ROOT = 0.7978845608028654
CUBE = 0.044715
ROWS, SUMS, LINE = 16, 24, 6
NN, NT = (((1,), (0,)), ((), ())), (((1,), (1,)), ((), ()))


def pieces(x, count):
    out = []
    for _ in range(count):
        top = x.astype(BF16)
        out.append(top)
        x = x - top.astype(F32)
    return out


def dot(a, b, dims, precision=None):
    return lax.dot_general(a, b, dims, precision=precision, preferred_element_type=F32)


def gelu_slope(x):
    sq = x * x
    th = jnp.tanh(ROOT * x * (1.0 + CUBE * sq))
    return 0.5 * (1.0 + th) + (0.5 * ROOT) * x * (1.0 - th * th) * (1.0 + 3.0 * CUBE * sq)


def pack_kernel(n, bases_ref, weight_ref, cot_ref, out_ref, hold):
    half = cot_ref.shape[0]
    share, channels = weight_ref.shape
    cols = channels // n
    for m in range(cols):
        hold[pl.ds(m, n, stride=LINE), :] = cot_ref[:, m * n : (m + 1) * n].astype(F32).T
    count = 2 * half
    place = lax.broadcasted_iota(jnp.int32, (count, count), 0)
    lane = lax.broadcasted_iota(jnp.int32, (count, count), 1)
    wanted = jnp.where(lane < half, 2 * lane, 2 * (lane - half) + 1)
    pick = (place == wanted).astype(BF16)
    row = bases_ref[...].astype(F32).astype(BF16)
    split = dot(jnp.broadcast_to(row, (8, count)), pick, NN)
    hold[pl.ds(3, n, stride=LINE), :] = jnp.broadcast_to(split[0:1, :half], (n, half))
    hold[pl.ds(4, n, stride=LINE), :] = jnp.broadcast_to(split[0:1, half:], (n, half))
    weight = weight_ref[...].astype(F32)
    rows = []
    for m in range(cols):
        rows += [weight[:, m * n : (m + 1) * n], jnp.zeros((ROWS - share, n), F32)]
    rows.append(jnp.zeros((half - cols * ROWS, n), F32))
    hold[pl.ds(5, n, stride=LINE), :] = jnp.concatenate(rows, axis=0).T
    out_ref[...] = hold[...].astype(BF16)


def main_kernel(
    seq, win, me_ref, got_ref, stem_ref, gain_ref, gained_ref, gram_ref, chosen_ref, turn_ref, out_ref, hold
):
    n = seq * win
    channels = stem_ref.shape[1]
    cols = channels // n
    lanes = seq * 128
    hold[: LINE * n, :] = got_ref[...].astype(F32)
    hold[LINE * n :, :] = jnp.zeros((8, 128), F32)
    chosen = chosen_ref[...]
    turn = turn_ref[...]

    own = hold[pl.ds(5, n, stride=LINE), :].T[: ROWS * cols]
    spread = dot(own.astype(BF16), chosen, NN)
    line = [
        jnp.sum(spread[ROWS * m : ROWS * (m + 1)] * turn, axis=0, keepdims=True)
        for m in range(cols)
    ]
    line = jnp.concatenate(line + [jnp.zeros_like(line[0])] * (4 - cols), axis=0)
    weights = jnp.concatenate(
        [line[:, t * channels : (t + 1) * channels] for t in range(KW)], axis=0
    ).astype(BF16)
    mixed = dot(weights, gained_ref[...], NT)
    mixed = mixed[:, 0:TAPS] + mixed[:, 24 : 24 + TAPS] + mixed[:, 48 : 48 + TAPS]
    blank = jnp.zeros((4, 4), F32)
    table = []
    for t in range(KW):
        tap = mixed[4 * t : 4 * t + 4]
        pair = [jnp.concatenate([tap, blank], axis=1), jnp.concatenate([blank, tap], axis=1)]
        table += pair if t % 2 == 0 else pair[::-1]
    table = [part.astype(F32) for part in pieces(jnp.concatenate(table, axis=0), 3)]
    table = jnp.concatenate([jnp.concatenate(table, axis=1), gram_ref[...]], axis=0).astype(BF16)

    sub = lax.broadcasted_iota(jnp.int32, (8, 128), 0)
    lane = lax.broadcasted_iota(jnp.int32, (8, lanes), 1)
    wide = lax.broadcasted_iota(jnp.int32, (8, lanes), 0)
    top = wide < 4
    first, last = lane == 0, lane == lanes - 1
    base = (wide % 4).astype(F32)

    def down(x, fill):
        return jnp.where(first, fill, pltpu.roll(x, 1, 1))

    def up(x, fill):
        return jnp.where(last, fill, pltpu.roll(x, lanes - 1, 1))

    total = jnp.zeros((96, 24), F32)
    for w in range(win):
        dr, mid = [], []
        for s in range(seq):
            at = LINE * (s * win + w)
            cell = jnp.where(sub < cols, 0.5 * hold[at : at + 8, :], 0.0)
            dr.append(cell + pltpu.roll(cell, 4, 0))
            mid.append(
                jnp.where(
                    sub < 4,
                    jnp.broadcast_to(hold[at + 3 : at + 4, :], (8, 128)),
                    jnp.broadcast_to(hold[at + 4 : at + 5, :], (8, 128)),
                )
            )
        dr, mid = jnp.concatenate(dr, axis=1), jnp.concatenate(mid, axis=1)
        hots = jnp.concatenate(
            [(cell == base).astype(F32) for cell in (down(mid, -1.0), mid, up(mid, -1.0))], axis=0
        )
        narrow = hots.astype(BF16)
        looked = dot(table, jnp.concatenate([narrow] * 3, axis=0), NN)
        taps = [looked[8 * t : 8 * t + 8] for t in range(KW)]
        mean_e = jnp.sum(looked[40:64] * hots, axis=0, keepdims=True)
        mean_o = jnp.sum(looked[64:88] * hots, axis=0, keepdims=True)
        scale_e = lax.rsqrt(mean_e + 1e-06)
        scale_o = lax.rsqrt(mean_o + 1e-06)
        scale = jnp.where(top, scale_e, scale_o)
        swapped = jnp.where(top, scale_o, scale_e)
        p0, p2, p4 = taps[0] * scale, taps[2] * scale, taps[4] * scale
        p1, p3 = taps[1] * swapped, taps[3] * swapped
        pre = down(p0 + jnp.where(top, p1, 0.0), 0.0)
        pre = pre + p2 + jnp.where(top, p3, p1)
        pre = pre + up(p4 + jnp.where(top, 0.0, p3), 0.0)
        dpre = dr * gelu_slope(pre)
        ahead, behind = up(dpre, 0.0), down(dpre, 0.0)
        d1 = jnp.where(top, ahead, dpre)
        d3 = jnp.where(top, dpre, behind)
        here = taps[0] * ahead + taps[2] * dpre + taps[4] * behind
        there = taps[1] * d1 + taps[3] * d3
        both = here + pltpu.roll(there, 4, 0)
        q_e = jnp.sum(jnp.where(top, both, 0.0), axis=0, keepdims=True)
        q_o = jnp.sum(jnp.where(top, 0.0, both), axis=0, keepdims=True)
        u_e = q_e * scale_e * scale_e * scale_e * (1.0 / channels)
        u_o = q_o * scale_o * scale_o * scale_o * (1.0 / channels)
        rows = [ahead * scale, d1 * swapped, dpre * scale, d3 * swapped, behind * scale, dr]
        rows = jnp.concatenate(rows + [hots * u_e, hots * u_o], axis=0)
        total = total + dot(rows.astype(BF16), narrow, NT)

    stem = stem_ref[...]
    gain = gain_ref[...]
    sums = []
    for t in range(KW + 1):
        cell = total[8 * t : 8 * t + 8]
        even, odd = (cell[0:4], cell[4:8]) if t % 2 == 0 or t == KW else (cell[4:8], cell[0:4])
        sums.append(even[:, :TAPS] + odd[:, 4:])
    grads = jnp.concatenate(sums[:KW], axis=0)
    crossed = total[48 : 48 + TAPS, :TAPS] + total[76:96, 4:]
    conv = dot(grads, stem * gain, NN, HIGH)
    conv = jnp.concatenate([conv[4 * t : 4 * t + 4] for t in range(KW)], axis=1)
    conv = jnp.concatenate([conv[m : m + 1] * turn for m in range(cols)], axis=0)
    conv = pieces(conv, 2)
    conv = dot(conv[0], chosen, NT) + dot(conv[1], chosen, NT)
    back = jnp.zeros((TAPS, channels), F32)
    for part in pieces(grads.T, 3):
        back = back + dot(part, weights, NN)
    stem_part = gain * back - dot(crossed, stem, NN, HIGH)
    gain_part = jnp.sum(stem * back, axis=0, keepdims=True)
    small = jnp.concatenate([stem_part, gain_part, jnp.zeros((3, channels), F32)], axis=0)
    direct = jnp.concatenate([sums[KW].T, jnp.zeros((4, 4), F32)], axis=0)
    mine = lax.broadcasted_iota(jnp.int32, (SUMS, n), 1) == me_ref[0]
    rows = [conv]
    for m in range(cols):
        rows.append(small[:, m * n : (m + 1) * n] + jnp.where(mine, direct[:, m : m + 1], 0.0))
    rows.append(jnp.zeros((128 - cols * (ROWS + SUMS), n), F32))
    out_ref[...] = jnp.concatenate(rows, axis=0).T


def finish_kernel(got_ref, stem_ref, gain_ref):
    n = got_ref.shape[0]
    turned = got_ref[...].T
    for m in range(stem_ref.shape[1] // n):
        stem_ref[:, m * n : (m + 1) * n] = turned[SUMS * m : SUMS * m + TAPS]
        gain_ref[:, m * n : (m + 1) * n] = turned[SUMS * m + TAPS : SUMS * m + TAPS + 1]


def call(kernel, name, out, operands, scratch=(), smem=0):
    space = [pl.BlockSpec(memory_space=pltpu.SMEM)] * smem
    space += [pl.BlockSpec(memory_space=pltpu.VMEM)] * (len(operands) - smem)
    many = isinstance(out, tuple)
    spec = pl.BlockSpec(memory_space=pltpu.VMEM)
    return pl.pallas_call(
        kernel,
        name=name,
        out_shape=out,
        in_specs=space,
        out_specs=(spec,) * len(out) if many else spec,
        scratch_shapes=list(scratch),
        compiler_params=pltpu.CompilerParams(vmem_limit_bytes=48 * 1024 * 1024),
    )(*operands)


def exchange(x):
    return lax.all_to_all(x, AXES, 0, 0, tiled=True)


def shards(bases, stem_weight, norm_gain, conv_weight, cotangent):
    seq, win = lax.axis_size("seq"), lax.axis_size("win")
    n = seq * win
    channels = norm_gain.shape[0]
    cols = channels // n
    half = bases.shape[1] // 2
    share = conv_weight.shape[0]
    me = lax.axis_index("seq") * win + lax.axis_index("win")

    sent = call(
        functools.partial(pack_kernel, n),
        "pack",
        jax.ShapeDtypeStruct((LINE * n, half), BF16),
        (bases, conv_weight, cotangent[0]),
        [pltpu.VMEM((LINE * n, half), F32)],
    )
    got = exchange(sent.reshape(n, LINE // 2, 2, half)).reshape(LINE * n, half)

    gained = stem_weight * norm_gain
    gained = [jnp.pad(part, ((0, 4), (0, 0))) for part in pieces(gained, 3)]
    gained = jnp.concatenate(gained, axis=0)
    gram = jnp.dot(stem_weight, stem_weight.T, precision=HIGH) * (1.0 / channels)
    gram = jnp.concatenate(
        [jnp.pad(gram, ((0, 4), (0, 4))), jnp.pad(gram, ((4, 0), (4, 0)))], axis=0
    )
    gram = jnp.concatenate([part.astype(F32) for part in pieces(gram, 3)], axis=1)
    row = jnp.arange(KW * channels, dtype=jnp.int32)[None, :]
    chosen = (row // share == jnp.arange(n, dtype=jnp.int32)[:, None]).astype(BF16)
    turn = (row % share == jnp.arange(ROWS, dtype=jnp.int32)[:, None]).astype(F32)

    packed = call(
        functools.partial(main_kernel, seq, win),
        "main",
        jax.ShapeDtypeStruct((n, 128), F32),
        (me.reshape(1), got, stem_weight, norm_gain[None], gained, gram, chosen, turn),
        [pltpu.VMEM((LINE * n + 8, 128), F32)],
        1,
    )
    got = exchange(packed)
    conv_grad = jnp.concatenate(
        [got[:, ROWS * m : ROWS * m + share].T for m in range(cols)], axis=1
    )
    mine = jnp.sum(got[:, cols * ROWS : cols * (ROWS + SUMS)], axis=0, keepdims=True)
    full = exchange(jnp.broadcast_to(mine, (n, mine.shape[1])))
    stem_grad, gain_grad = call(
        finish_kernel,
        "finish",
        (
            jax.ShapeDtypeStruct((TAPS, channels), F32),
            jax.ShapeDtypeStruct((1, channels), F32),
        ),
        (full,),
    )
    return (conv_grad, stem_grad, gain_grad[0])


def solution(mesh):
    in_specs = (P("win", "seq"), P(), P(), P(("seq", "win"), None), P("win", "seq", None))
    out_specs = (P(("seq", "win"), None), P(), P())
    return jax.shard_map(shards, mesh=mesh, in_specs=in_specs, out_specs=out_specs, check_vma=False)
```

```python
import functools

import jax
import jax.numpy as jnp
from jax import lax
from jax.experimental import pallas as pl
from jax.experimental.pallas import tpu as pltpu
from jax.sharding import PartitionSpec as P

KW = 5
TAPS = 4 * KW
AXES = ("seq", "win")
F32 = jnp.float32
BF16 = jnp.bfloat16
HIGH = lax.Precision.HIGHEST
ROOT = 0.7978845608028654
CUBE = 0.044715
ROWS, SUMS, LINE = 16, 24, 6
CELLS = 4
NN, NT = (((1,), (0,)), ((), ())), (((1,), (1,)), ((), ()))


def pieces(x, count):
    out = []
    for _ in range(count):
        top = x.astype(BF16)
        out.append(top)
        x = x - top.astype(F32)
    return out


def dot(a, b, dims, precision=None):
    return lax.dot_general(a, b, dims, precision=precision, preferred_element_type=F32)


def gelu_slope(x):
    sq = x * x
    th = jnp.tanh(ROOT * x * (1.0 + CUBE * sq))
    return 0.5 * (1.0 + th) + (0.5 * ROOT) * x * (1.0 - th * th) * (1.0 + 3.0 * CUBE * sq)


def pack_kernel(n, bases_hbm, weight_hbm, cot_hbm, out_ref, bases_ref, weight_ref, cot_ref, hold, sems):
    copies = [
        pltpu.make_async_copy(*pair, sems.at[i])
        for i, pair in enumerate(
            ((cot_hbm, cot_ref), (weight_hbm, weight_ref), (bases_hbm, bases_ref))
        )
    ]
    for copy in copies:
        copy.start()
    for copy in copies:
        copy.wait()
    half = cot_ref.shape[0]
    share, channels = weight_ref.shape
    cols = channels // n
    for m in range(cols):
        hold[pl.ds(m, n, stride=LINE), :] = cot_ref[:, m * n : (m + 1) * n].astype(F32).T
    count = 2 * half
    place = lax.broadcasted_iota(jnp.int32, (count, count), 0)
    lane = lax.broadcasted_iota(jnp.int32, (count, count), 1)
    wanted = jnp.where(lane < half, 2 * lane, 2 * (lane - half) + 1)
    pick = (place == wanted).astype(BF16)
    row = bases_ref[...].astype(F32).astype(BF16)
    split = dot(jnp.broadcast_to(row, (8, count)), pick, NN)
    hold[pl.ds(3, n, stride=LINE), :] = jnp.broadcast_to(split[0:1, :half], (n, half))
    hold[pl.ds(4, n, stride=LINE), :] = jnp.broadcast_to(split[0:1, half:], (n, half))
    weight = weight_ref[...].astype(F32)
    rows = []
    for m in range(cols):
        rows += [weight[:, m * n : (m + 1) * n], jnp.zeros((ROWS - share, n), F32)]
    rows.append(jnp.zeros((half - cols * ROWS, n), F32))
    hold[pl.ds(5, n, stride=LINE), :] = jnp.concatenate(rows, axis=0).T
    out_ref[...] = hold[...].astype(BF16)


def main_kernel(
    seq, win, me_ref, got_ref, stem_ref, gain_ref, gained_ref, gram_ref, chosen_ref, turn_ref, out_ref, hold
):
    n = seq * win
    channels = stem_ref.shape[1]
    cols = channels // n
    hold[: LINE * n, :] = got_ref[...].astype(F32)
    hold[LINE * n :, :] = jnp.zeros((8, 128), F32)
    chosen = chosen_ref[...]
    turn = turn_ref[...]

    own = hold[pl.ds(5, n, stride=LINE), :].T[: ROWS * cols]
    spread = dot(own.astype(BF16), chosen, NN)
    line = [
        jnp.sum(spread[ROWS * m : ROWS * (m + 1)] * turn, axis=0, keepdims=True)
        for m in range(cols)
    ]
    line = jnp.concatenate(line + [jnp.zeros_like(line[0])] * (4 - cols), axis=0)
    weights = jnp.concatenate(
        [line[:, t * channels : (t + 1) * channels] for t in range(KW)], axis=0
    ).astype(BF16)
    mixed = dot(weights, gained_ref[...], NT)
    mixed = mixed[:, 0:TAPS] + mixed[:, 24 : 24 + TAPS] + mixed[:, 48 : 48 + TAPS]
    blank = jnp.zeros((4, 4), F32)
    table = []
    for t in range(KW):
        tap = mixed[4 * t : 4 * t + 4]
        pair = [jnp.concatenate([tap, blank], axis=1), jnp.concatenate([blank, tap], axis=1)]
        table += pair if t % 2 == 0 else pair[::-1]
    table = [part.astype(F32) for part in pieces(jnp.concatenate(table, axis=0), 3)]
    table = jnp.concatenate([jnp.concatenate(table, axis=1), jnp.zeros((32, 72), F32)], axis=0)
    table = (table + gram_ref[...]).astype(BF16)

    width = 128 * CELLS
    count = seq // CELLS
    sub = lax.broadcasted_iota(jnp.int32, (8, 128), 0)
    lane = lax.broadcasted_iota(jnp.int32, (8, width), 1)
    wide = lax.broadcasted_iota(jnp.int32, (8, width), 0)
    top = wide < 4
    first, last = lane == 0, lane == width - 1
    base = (wide % 4).astype(F32)

    def ahead_of(x):
        return pltpu.roll(x, width - 1, 1)

    def behind_of(x):
        return pltpu.roll(x, 1, 1)

    def load(w, c):
        dr, mid = [], []
        for s in range(c * CELLS, (c + 1) * CELLS):
            at = LINE * (s * win + w)
            cell = jnp.where(sub < cols, 0.5 * hold[at : at + 8, :], 0.0)
            dr.append(cell + pltpu.roll(cell, 4, 0))
            mid.append(
                jnp.where(
                    sub < 4,
                    jnp.broadcast_to(hold[at + 3 : at + 4, :], (8, 128)),
                    jnp.broadcast_to(hold[at + 4 : at + 5, :], (8, 128)),
                )
            )
        mid = jnp.concatenate(mid, axis=1)
        return jnp.concatenate(dr, axis=1), mid, ahead_of(mid), behind_of(mid)

    def look(prior, cell, later):
        dr, mid, left, right = cell
        down = jnp.where(first, -1.0 if prior is None else prior[3], right)
        up = jnp.where(last, -1.0 if later is None else later[2], left)
        hots = jnp.concatenate([(x == base).astype(F32) for x in (down, mid, up)], axis=0)
        narrow = hots.astype(BF16)
        looked = dot(table, jnp.concatenate([narrow] * 3, axis=0), NN)
        taps = [looked[8 * t : 8 * t + 8] for t in range(KW)]
        mean_e = jnp.sum(looked[40:56] * hots[0:16], axis=0, keepdims=True) + looked[3:4]
        mean_o = jnp.sum(looked[56:72] * hots[8:24], axis=0, keepdims=True) + looked[7:8]
        scale_e = lax.rsqrt(mean_e + 1e-06)
        scale_o = lax.rsqrt(mean_o + 1e-06)
        scale = jnp.where(top, scale_e, scale_o)
        swapped = jnp.where(top, scale_o, scale_e)
        p0, p2, p4 = taps[0] * scale, taps[2] * scale, taps[4] * scale
        p1, p3 = taps[1] * swapped, taps[3] * swapped
        down = behind_of(p0 + jnp.where(top, p1, 0.0))
        up = ahead_of(p4 + jnp.where(top, 0.0, p3))
        return (p2 + jnp.where(top, p3, p1), up, down), (
            hots, narrow, taps, scale_e, scale_o, scale, swapped, dr
        )

    def slope(prior, cell, later, dr):
        pre = cell[0] + jnp.where(first, 0.0 if prior is None else prior[2], cell[2])
        pre = pre + jnp.where(last, 0.0 if later is None else later[1], cell[1])
        dpre = dr * gelu_slope(pre)
        return dpre, ahead_of(dpre), behind_of(dpre)

    def close(prior, cell, later, kept):
        hots, narrow, taps, scale_e, scale_o, scale, swapped, dr = kept
        dpre = cell[0]
        ahead = jnp.where(last, 0.0 if later is None else later[1], cell[1])
        behind = jnp.where(first, 0.0 if prior is None else prior[2], cell[2])
        d1 = jnp.where(top, ahead, dpre)
        d3 = jnp.where(top, dpre, behind)
        here = taps[0] * ahead + taps[2] * dpre + taps[4] * behind
        there = taps[1] * d1 + taps[3] * d3
        both = here + pltpu.roll(there, 4, 0)
        q_e = jnp.sum(jnp.where(top, both, 0.0), axis=0, keepdims=True)
        q_o = jnp.sum(jnp.where(top, 0.0, both), axis=0, keepdims=True)
        u_e = q_e * scale_e * scale_e * scale_e * (1.0 / channels)
        u_o = q_o * scale_o * scale_o * scale_o * (1.0 / channels)
        lead = jnp.where(wide == 3, u_e, jnp.where(wide == 7, u_o, ahead * scale))
        rows = [lead, d1 * swapped, dpre * scale, d3 * swapped, behind * scale, dr]
        rows = jnp.concatenate(rows, axis=0).astype(BF16)
        u_e, u_o = u_e.astype(BF16) * narrow[0:16], u_o.astype(BF16) * hots[8:24].astype(BF16)
        return dot(jnp.concatenate([rows, u_e, u_o], axis=0), narrow, NT)

    def at(items, i):
        return items[i] if 0 <= i < len(items) else None

    total = jnp.zeros((80, 24), F32)
    for w in range(win):
        loaded, looked, kept, slopes = [load(w, 0)], [], [], []
        for step in range(count + 2):
            if step + 1 < count:
                loaded.append(load(w, step + 1))
            if step < count:
                part, keep = look(at(loaded, step - 1), loaded[step], at(loaded, step + 1))
                looked.append(part)
                kept.append(keep)
            if 0 <= step - 1 < count:
                c = step - 1
                slopes.append(slope(at(looked, c - 1), looked[c], at(looked, c + 1), kept[c][7]))
            if 0 <= step - 2 < count:
                c = step - 2
                total = total + close(at(slopes, c - 1), slopes[c], at(slopes, c + 1), kept[c])

    stem = stem_ref[...]
    gain = gain_ref[...]
    sums = []
    for t in range(KW + 1):
        cell = total[8 * t : 8 * t + 8]
        even, odd = (cell[0:4], cell[4:8]) if t % 2 == 0 or t == KW else (cell[4:8], cell[0:4])
        sums.append(even[:, :TAPS] + odd[:, 4:])
    grads = jnp.concatenate(sums[:KW], axis=0)
    even, odd = total[48:64, :TAPS], total[64:80, 4:]
    same = lax.broadcasted_iota(jnp.int32, (4, 4), 0) == lax.broadcasted_iota(jnp.int32, (4, 4), 1)
    even_end = [even[:, 16:].T, jnp.where(same, total[3:4, 16:TAPS], 0.0)]
    odd_end = [jnp.where(same, total[7:8, 4:8], 0.0), odd[:, :4].T]
    crossed = jnp.concatenate([even, jnp.concatenate(even_end, axis=1)], axis=0)
    crossed = crossed + jnp.concatenate([jnp.concatenate(odd_end, axis=1), odd], axis=0)
    conv = dot(grads, stem * gain, NN, HIGH)
    conv = jnp.concatenate([conv[4 * t : 4 * t + 4] for t in range(KW)], axis=1)
    conv = jnp.concatenate([conv[m : m + 1] * turn for m in range(cols)], axis=0)
    conv = dot(jnp.concatenate(pieces(conv, 2), axis=0), chosen, NT)
    conv = conv[: ROWS * cols] + conv[ROWS * cols :]
    back = jnp.zeros((TAPS, channels), F32)
    for part in pieces(grads.T, 3):
        back = back + dot(part, weights, NN)
    stem_part = gain * back - dot(crossed, stem, NN, HIGH)
    gain_part = jnp.sum(stem * back, axis=0, keepdims=True)
    small = jnp.concatenate([stem_part, gain_part, jnp.zeros((3, channels), F32)], axis=0)
    direct = jnp.concatenate([sums[KW].T, jnp.zeros((4, 4), F32)], axis=0)
    mine = lax.broadcasted_iota(jnp.int32, (SUMS, n), 1) == me_ref[0]
    rows = [conv]
    for m in range(cols):
        rows.append(small[:, m * n : (m + 1) * n] + jnp.where(mine, direct[:, m : m + 1], 0.0))
    rows.append(jnp.zeros((128 - cols * (ROWS + SUMS), n), F32))
    out_ref[...] = jnp.concatenate(rows, axis=0).T


def reduce_kernel(got_ref, out_ref):
    out_ref[...] = jnp.broadcast_to(jnp.sum(got_ref[...], axis=0, keepdims=True), out_ref.shape)


def finish_kernel(got_ref, stem_ref, gain_ref):
    n = got_ref.shape[0]
    cols = stem_ref.shape[1] // n
    turned = got_ref[...].T
    for m in range(cols):
        at = ROWS * cols + SUMS * m
        stem_ref[:, m * n : (m + 1) * n] = turned[at : at + TAPS]
        gain_ref[m * n : (m + 1) * n] = turned[at + TAPS]


def call(kernel, name, out, operands, scratch=(), smem=0, space=pltpu.VMEM, limit=48):
    specs = [pl.BlockSpec(memory_space=pltpu.SMEM)] * smem
    specs += [pl.BlockSpec(memory_space=space)] * (len(operands) - smem)
    many = isinstance(out, tuple)
    spec = pl.BlockSpec(memory_space=pltpu.VMEM)
    return pl.pallas_call(
        kernel,
        name=name,
        out_shape=out,
        in_specs=specs,
        out_specs=(spec,) * len(out) if many else spec,
        scratch_shapes=list(scratch),
        compiler_params=pltpu.CompilerParams(vmem_limit_bytes=limit * 1024 * 1024),
    )(*operands)


def exchange(x):
    return lax.all_to_all(x, AXES, 0, 0, tiled=True)


def shards(bases, stem_weight, norm_gain, conv_weight, cotangent):
    seq, win = lax.axis_size("seq"), lax.axis_size("win")
    n = seq * win
    channels = norm_gain.shape[0]
    cols = channels // n
    half = bases.shape[1] // 2
    share = conv_weight.shape[0]
    me = lax.axis_index("seq") * win + lax.axis_index("win")

    sent = call(
        functools.partial(pack_kernel, n),
        "pack",
        jax.ShapeDtypeStruct((LINE * n, half), BF16),
        (bases, conv_weight, cotangent[0]),
        [
            pltpu.VMEM(bases.shape, jnp.int32),
            pltpu.VMEM(conv_weight.shape, BF16),
            pltpu.VMEM(cotangent.shape[1:], BF16),
            pltpu.VMEM((LINE * n, half), F32),
            pltpu.SemaphoreType.DMA((3,)),
        ],
        space=pltpu.HBM,
        limit=60,
    )
    got = exchange(sent.reshape(n, LINE // 2, 2, half)).reshape(LINE * n, half)

    gained = stem_weight * norm_gain
    gained = [jnp.pad(part, ((0, 4), (0, 0))) for part in pieces(gained, 3)]
    gained = jnp.concatenate(gained, axis=0)
    gram = jnp.dot(stem_weight, stem_weight.T, precision=HIGH) * (1.0 / channels)
    tap = jnp.arange(TAPS) // 4
    ahead, same = tap[None] > tap[:, None], tap[None] == tap[:, None]
    even = jnp.pad(gram * (2.0 * ahead + same), ((0, 0), (0, 4)))
    odd = jnp.pad(gram * (2.0 * ahead.T + same), ((0, 0), (4, 0)))
    ends = jnp.diag(gram)
    lines = jnp.arange(8 * KW)[:, None]
    ends = jnp.where(lines == 3, jnp.pad(ends, (0, 4)) * (jnp.arange(24) >= 16), 0.0) + jnp.where(
        lines == 7, jnp.pad(ends, (4, 0)) * (jnp.arange(24) < 8), 0.0
    )
    gram = jnp.concatenate([ends, even[:16], odd[4:]], axis=0)
    gram = jnp.concatenate([part.astype(F32) for part in pieces(gram, 3)], axis=1)
    row = jnp.arange(KW * channels, dtype=jnp.int32)[None, :]
    chosen = (row // share == jnp.arange(n, dtype=jnp.int32)[:, None]).astype(BF16)
    turn = (row % share == jnp.arange(ROWS, dtype=jnp.int32)[:, None]).astype(F32)

    packed = call(
        functools.partial(main_kernel, seq, win),
        "main",
        jax.ShapeDtypeStruct((n, 128), F32),
        (me.reshape(1), got, stem_weight, norm_gain[None], gained, gram, chosen, turn),
        [pltpu.VMEM((LINE * n + 8, 128), F32)],
        1,
    )
    got = exchange(packed)
    conv_grad = jnp.concatenate(
        [got[:, ROWS * m : ROWS * m + share].T for m in range(cols)], axis=1
    )
    mine = call(reduce_kernel, "reduce", jax.ShapeDtypeStruct((n, 128), F32), (got,))
    full = exchange(mine)
    stem_grad, gain_grad = call(
        finish_kernel,
        "finish",
        (
            jax.ShapeDtypeStruct((TAPS, channels), F32),
            jax.ShapeDtypeStruct((channels,), F32),
        ),
        (full,),
    )
    return (conv_grad, stem_grad, gain_grad)


def solution(mesh):
    in_specs = (P("win", "seq"), P(), P(), P(("seq", "win"), None), P("win", "seq", None))
    out_specs = (P(("seq", "win"), None), P(), P())
    return jax.shard_map(shards, mesh=mesh, in_specs=in_specs, out_specs=out_specs, check_vma=False)
```

```python
import functools

import jax
import jax.numpy as jnp
from jax import lax
from jax.experimental import pallas as pl
from jax.experimental.pallas import tpu as pltpu
from jax.sharding import Mesh, PartitionSpec as P

KW = 5
TAPS = 4 * KW
PLANE = ("row", "win")
AXES = ("layer",) + PLANE
F32 = jnp.float32
BF16 = jnp.bfloat16
HIGH = lax.Precision.HIGHEST
ROOT = 0.7978845608028654
CUBE = 0.044715
ROWS, SUMS, LINE = 16, 24, 6
CELLS = 4
LAYERS = 8
NN, NT = (((1,), (0,)), ((), ())), (((1,), (1,)), ((), ()))


def pieces(x, count):
    out = []
    for _ in range(count):
        top = x.astype(BF16)
        out.append(top)
        x = x - top.astype(F32)
    return out


def dot(a, b, dims, precision=None):
    return lax.dot_general(a, b, dims, precision=precision, preferred_element_type=F32)


def gelu_slope(x):
    sq = x * x
    th = jnp.tanh(ROOT * x * (1.0 + CUBE * sq))
    return 0.5 * (1.0 + th) + (0.5 * ROOT) * x * (1.0 - th * th) * (1.0 + 3.0 * CUBE * sq)


def pack_kernel(n, bases_hbm, weight_hbm, cot_hbm, out_ref, bases_ref, weight_ref, cot_ref, hold, sems):
    copies = [
        pltpu.make_async_copy(*pair, sems.at[i])
        for i, pair in enumerate(
            ((cot_hbm, cot_ref), (weight_hbm, weight_ref), (bases_hbm, bases_ref))
        )
    ]
    for copy in copies:
        copy.start()
    for copy in copies:
        copy.wait()
    half = cot_ref.shape[0]
    share, channels = weight_ref.shape
    cols = channels // n
    for m in range(cols):
        hold[pl.ds(m, n, stride=LINE), :] = cot_ref[:, m * n : (m + 1) * n].astype(F32).T
    count = 2 * half
    place = lax.broadcasted_iota(jnp.int32, (count, count), 0)
    lane = lax.broadcasted_iota(jnp.int32, (count, count), 1)
    wanted = jnp.where(lane < half, 2 * lane, 2 * (lane - half) + 1)
    pick = (place == wanted).astype(BF16)
    row = bases_ref[...].astype(F32).astype(BF16)
    split = dot(jnp.broadcast_to(row, (8, count)), pick, NN)
    hold[pl.ds(3, n, stride=LINE), :] = jnp.broadcast_to(split[0:1, :half], (n, half))
    hold[pl.ds(4, n, stride=LINE), :] = jnp.broadcast_to(split[0:1, half:], (n, half))
    weight = weight_ref[...].astype(F32)
    rows = []
    for m in range(cols):
        rows += [weight[:, m * n : (m + 1) * n], jnp.zeros((ROWS - share, n), F32)]
    rows.append(jnp.zeros((half - cols * ROWS, n), F32))
    hold[pl.ds(5, n, stride=LINE), :] = jnp.concatenate(rows, axis=0).T
    out_ref[...] = hold[...].astype(BF16)


def main_kernel(
    layers, seq, win, me_ref, got_ref, stem_ref, gain_ref, gained_ref, gram_ref, chosen_ref, turn_ref, out_ref, hold
):
    n = seq * win
    plane = n // layers
    channels = stem_ref.shape[1]
    cols = channels // n
    hold[: LINE * n, :] = got_ref[...].astype(F32)
    hold[LINE * n :, :] = jnp.zeros((8, 128), F32)
    chosen = chosen_ref[...]
    turn = turn_ref[...]

    own = hold[pl.ds(5, n, stride=LINE), :].T[: ROWS * cols]
    spread = dot(own.astype(BF16), chosen, NN)
    line = [
        jnp.sum(spread[ROWS * m : ROWS * (m + 1)] * turn, axis=0, keepdims=True)
        for m in range(cols)
    ]
    line = jnp.concatenate(line + [jnp.zeros_like(line[0])] * (4 - cols), axis=0)
    weights = jnp.concatenate(
        [line[:, t * channels : (t + 1) * channels] for t in range(KW)], axis=0
    ).astype(BF16)
    mixed = dot(weights, gained_ref[...], NT)
    mixed = mixed[:, 0:TAPS] + mixed[:, 24 : 24 + TAPS] + mixed[:, 48 : 48 + TAPS]
    blank = jnp.zeros((4, 4), F32)
    table = []
    for t in range(KW):
        tap = mixed[4 * t : 4 * t + 4]
        pair = [jnp.concatenate([tap, blank], axis=1), jnp.concatenate([blank, tap], axis=1)]
        table += pair if t % 2 == 0 else pair[::-1]
    table = [part.astype(F32) for part in pieces(jnp.concatenate(table, axis=0), 3)]
    table = jnp.concatenate([jnp.concatenate(table, axis=1), jnp.zeros((32, 72), F32)], axis=0)
    table = (table + gram_ref[...]).astype(BF16)

    width = 128 * CELLS
    count = seq // CELLS
    sub = lax.broadcasted_iota(jnp.int32, (8, 128), 0)
    lane = lax.broadcasted_iota(jnp.int32, (8, width), 1)
    wide = lax.broadcasted_iota(jnp.int32, (8, width), 0)
    top = wide < 4
    first, last = lane == 0, lane == width - 1
    base = (wide % 4).astype(F32)

    def ahead_of(x):
        return pltpu.roll(x, width - 1, 1)

    def behind_of(x):
        return pltpu.roll(x, 1, 1)

    def load(w, c):
        dr, mid = [], []
        for s in range(c * CELLS, (c + 1) * CELLS):
            at = LINE * (s * win + w)
            cell = jnp.where(sub < cols, 0.5 * hold[at : at + 8, :], 0.0)
            dr.append(cell + pltpu.roll(cell, 4, 0))
            mid.append(
                jnp.where(
                    sub < 4,
                    jnp.broadcast_to(hold[at + 3 : at + 4, :], (8, 128)),
                    jnp.broadcast_to(hold[at + 4 : at + 5, :], (8, 128)),
                )
            )
        mid = jnp.concatenate(mid, axis=1)
        return jnp.concatenate(dr, axis=1), mid, ahead_of(mid), behind_of(mid)

    def look(prior, cell, later):
        dr, mid, left, right = cell
        down = jnp.where(first, -1.0 if prior is None else prior[3], right)
        up = jnp.where(last, -1.0 if later is None else later[2], left)
        hots = jnp.concatenate([(x == base).astype(F32) for x in (down, mid, up)], axis=0)
        narrow = hots.astype(BF16)
        looked = dot(table, jnp.concatenate([narrow] * 3, axis=0), NN)
        taps = [looked[8 * t : 8 * t + 8] for t in range(KW)]
        mean_e = jnp.sum(looked[40:56] * hots[0:16], axis=0, keepdims=True) + looked[3:4]
        mean_o = jnp.sum(looked[56:72] * hots[8:24], axis=0, keepdims=True) + looked[7:8]
        scale_e = lax.rsqrt(mean_e + 1e-06)
        scale_o = lax.rsqrt(mean_o + 1e-06)
        scale = jnp.where(top, scale_e, scale_o)
        swapped = jnp.where(top, scale_o, scale_e)
        p0, p2, p4 = taps[0] * scale, taps[2] * scale, taps[4] * scale
        p1, p3 = taps[1] * swapped, taps[3] * swapped
        down = behind_of(p0 + jnp.where(top, p1, 0.0))
        up = ahead_of(p4 + jnp.where(top, 0.0, p3))
        return (p2 + jnp.where(top, p3, p1), up, down), (
            hots, narrow, taps, scale_e, scale_o, scale, swapped, dr
        )

    def slope(prior, cell, later, dr):
        pre = cell[0] + jnp.where(first, 0.0 if prior is None else prior[2], cell[2])
        pre = pre + jnp.where(last, 0.0 if later is None else later[1], cell[1])
        dpre = dr * gelu_slope(pre)
        return dpre, ahead_of(dpre), behind_of(dpre)

    def close(prior, cell, later, kept):
        hots, narrow, taps, scale_e, scale_o, scale, swapped, dr = kept
        dpre = cell[0]
        ahead = jnp.where(last, 0.0 if later is None else later[1], cell[1])
        behind = jnp.where(first, 0.0 if prior is None else prior[2], cell[2])
        d1 = jnp.where(top, ahead, dpre)
        d3 = jnp.where(top, dpre, behind)
        here = taps[0] * ahead + taps[2] * dpre + taps[4] * behind
        there = taps[1] * d1 + taps[3] * d3
        both = here + pltpu.roll(there, 4, 0)
        q_e = jnp.sum(jnp.where(top, both, 0.0), axis=0, keepdims=True)
        q_o = jnp.sum(jnp.where(top, 0.0, both), axis=0, keepdims=True)
        u_e = q_e * scale_e * scale_e * scale_e * (1.0 / channels)
        u_o = q_o * scale_o * scale_o * scale_o * (1.0 / channels)
        lead = jnp.where(wide == 3, u_e, jnp.where(wide == 7, u_o, ahead * scale))
        rows = [lead, d1 * swapped, dpre * scale, d3 * swapped, behind * scale, dr]
        rows = jnp.concatenate(rows, axis=0).astype(BF16)
        u_e, u_o = u_e.astype(BF16) * narrow[0:16], u_o.astype(BF16) * hots[8:24].astype(BF16)
        return dot(jnp.concatenate([rows, u_e, u_o], axis=0), narrow, NT)

    def at(items, i):
        return items[i] if 0 <= i < len(items) else None

    total = jnp.zeros((80, 24), F32)
    for w in range(win):
        loaded, looked, kept, slopes = [load(w, 0)], [], [], []
        for step in range(count + 2):
            if step + 1 < count:
                loaded.append(load(w, step + 1))
            if step < count:
                part, keep = look(at(loaded, step - 1), loaded[step], at(loaded, step + 1))
                looked.append(part)
                kept.append(keep)
            if 0 <= step - 1 < count:
                c = step - 1
                slopes.append(slope(at(looked, c - 1), looked[c], at(looked, c + 1), kept[c][7]))
            if 0 <= step - 2 < count:
                c = step - 2
                total = total + close(at(slopes, c - 1), slopes[c], at(slopes, c + 1), kept[c])

    stem = stem_ref[...]
    gain = gain_ref[...]
    sums = []
    for t in range(KW + 1):
        cell = total[8 * t : 8 * t + 8]
        even, odd = (cell[0:4], cell[4:8]) if t % 2 == 0 or t == KW else (cell[4:8], cell[0:4])
        sums.append(even[:, :TAPS] + odd[:, 4:])
    grads = jnp.concatenate(sums[:KW], axis=0)
    even, odd = total[48:64, :TAPS], total[64:80, 4:]
    same = lax.broadcasted_iota(jnp.int32, (4, 4), 0) == lax.broadcasted_iota(jnp.int32, (4, 4), 1)
    even_end = [even[:, 16:].T, jnp.where(same, total[3:4, 16:TAPS], 0.0)]
    odd_end = [jnp.where(same, total[7:8, 4:8], 0.0), odd[:, :4].T]
    crossed = jnp.concatenate([even, jnp.concatenate(even_end, axis=1)], axis=0)
    crossed = crossed + jnp.concatenate([jnp.concatenate(odd_end, axis=1), odd], axis=0)
    conv = dot(grads, stem * gain, NN, HIGH)
    conv = jnp.concatenate([conv[4 * t : 4 * t + 4] for t in range(KW)], axis=1)
    conv = jnp.concatenate([conv[m : m + 1] * turn for m in range(cols)], axis=0)
    conv = dot(jnp.concatenate(pieces(conv, 2), axis=0), chosen, NT)
    conv = conv[: ROWS * cols] + conv[ROWS * cols :]
    back = jnp.zeros((TAPS, channels), F32)
    for part in pieces(grads.T, 3):
        back = back + dot(part, weights, NN)
    stem_part = gain * back - dot(crossed, stem, NN, HIGH)
    gain_part = jnp.sum(stem * back, axis=0, keepdims=True)
    small = jnp.concatenate([stem_part, gain_part, jnp.zeros((3, channels), F32)], axis=0)
    direct = jnp.concatenate([sums[KW].T, jnp.zeros((4, 4), F32)], axis=0)
    mine = lax.broadcasted_iota(jnp.int32, (SUMS, n), 1) == me_ref[0]
    rows = [conv]
    for m in range(cols):
        rows.append(small[:, m * n : (m + 1) * n] + jnp.where(mine, direct[:, m : m + 1], 0.0))
    rows.append(jnp.zeros((128 - cols * (ROWS + SUMS), n), F32))
    rows = jnp.concatenate(rows, axis=0).T
    for layer in range(layers):
        out_ref[pl.ds(layer, plane, stride=layers), :] = rows[layer * plane : (layer + 1) * plane]


def relay_kernel(layers, first, got_ref, out_ref):
    plane = got_ref.shape[0] // layers
    total = got_ref[0:layers, :]
    for source in range(1, plane):
        total = total + got_ref[source * layers : (source + 1) * layers, :]
    lane = lax.broadcasted_iota(jnp.int32, total.shape, 1)
    for layer in range(layers):
        rows = got_ref[pl.ds(layer, plane, stride=layers), :]
        at = layer * plane
        out_ref[at : at + layers, :] = jnp.where(lane < first, rows[:layers], total)
        out_ref[at + layers : at + plane, :] = rows[layers:]


def total_kernel(layers, got_ref, out_ref):
    plane = got_ref.shape[0] // layers
    total = got_ref[0:layers, :]
    for layer in range(1, layers):
        total = total + got_ref[layer * plane : layer * plane + layers, :]
    for target in range(plane):
        out_ref[target * layers : (target + 1) * layers, :] = total


def finish_kernel(layers, got_ref, stem_ref, gain_ref):
    n = got_ref.shape[0]
    cols = stem_ref.shape[1] // n
    turned = [got_ref[pl.ds(layer, n // layers, stride=layers), :] for layer in range(layers)]
    turned = jnp.concatenate(turned, axis=0).T
    for m in range(cols):
        at = ROWS * cols + SUMS * m
        stem_ref[:, m * n : (m + 1) * n] = turned[at : at + TAPS]
        gain_ref[m * n : (m + 1) * n] = turned[at + TAPS]


def call(kernel, name, out, operands, scratch=(), smem=0, space=pltpu.VMEM, limit=48):
    specs = [pl.BlockSpec(memory_space=pltpu.SMEM)] * smem
    specs += [pl.BlockSpec(memory_space=space)] * (len(operands) - smem)
    many = isinstance(out, tuple)
    spec = pl.BlockSpec(memory_space=pltpu.VMEM)
    return pl.pallas_call(
        kernel,
        name=name,
        out_shape=out,
        in_specs=specs,
        out_specs=(spec,) * len(out) if many else spec,
        scratch_shapes=list(scratch),
        compiler_params=pltpu.CompilerParams(vmem_limit_bytes=limit * 1024 * 1024),
    )(*operands)


def exchange(x, axes):
    return lax.all_to_all(x, axes, 0, 0, tiled=True)


def shards(bases, stem_weight, norm_gain, conv_weight, cotangent):
    layers, win = lax.axis_size("layer"), lax.axis_size("win")
    seq = layers * lax.axis_size("row")
    n = seq * win
    plane = n // layers
    channels = norm_gain.shape[0]
    cols = channels // n
    half = bases.shape[1] // 2
    share = conv_weight.shape[0]
    me = lax.axis_index(AXES)

    sent = call(
        functools.partial(pack_kernel, n),
        "pack",
        jax.ShapeDtypeStruct((LINE * n, half), BF16),
        (bases, conv_weight, cotangent[0]),
        [
            pltpu.VMEM(bases.shape, jnp.int32),
            pltpu.VMEM(conv_weight.shape, BF16),
            pltpu.VMEM(cotangent.shape[1:], BF16),
            pltpu.VMEM((LINE * n, half), F32),
            pltpu.SemaphoreType.DMA((3,)),
        ],
        space=pltpu.HBM,
        limit=60,
    )
    got = exchange(sent.reshape(n, LINE // 2, 2, half), AXES).reshape(LINE * n, half)

    gained = stem_weight * norm_gain
    gained = [jnp.pad(part, ((0, 4), (0, 0))) for part in pieces(gained, 3)]
    gained = jnp.concatenate(gained, axis=0)
    gram = jnp.dot(stem_weight, stem_weight.T, precision=HIGH) * (1.0 / channels)
    tap = jnp.arange(TAPS) // 4
    ahead, same = tap[None] > tap[:, None], tap[None] == tap[:, None]
    even = jnp.pad(gram * (2.0 * ahead + same), ((0, 0), (0, 4)))
    odd = jnp.pad(gram * (2.0 * ahead.T + same), ((0, 0), (4, 0)))
    ends = jnp.diag(gram)
    lines = jnp.arange(8 * KW)[:, None]
    ends = jnp.where(lines == 3, jnp.pad(ends, (0, 4)) * (jnp.arange(24) >= 16), 0.0) + jnp.where(
        lines == 7, jnp.pad(ends, (4, 0)) * (jnp.arange(24) < 8), 0.0
    )
    gram = jnp.concatenate([ends, even[:16], odd[4:]], axis=0)
    gram = jnp.concatenate([part.astype(F32) for part in pieces(gram, 3)], axis=1)
    row = jnp.arange(KW * channels, dtype=jnp.int32)[None, :]
    chosen = (row // share == jnp.arange(n, dtype=jnp.int32)[:, None]).astype(BF16)
    turn = (row % share == jnp.arange(ROWS, dtype=jnp.int32)[:, None]).astype(F32)

    packed = call(
        functools.partial(main_kernel, layers, seq, win),
        "main",
        jax.ShapeDtypeStruct((n, 128), F32),
        (me.reshape(1), got, stem_weight, norm_gain[None], gained, gram, chosen, turn),
        [pltpu.VMEM((LINE * n + 8, 128), F32)],
        1,
    )
    shape = jax.ShapeDtypeStruct((n, 128), F32)
    got = exchange(packed.reshape(plane, layers, 128), PLANE).reshape(n, 128)
    relayed = call(functools.partial(relay_kernel, layers, cols * ROWS), "relay", shape, (got,))
    got = exchange(relayed.reshape(layers, plane, 128), "layer").reshape(n, 128)
    conv_grad = jnp.concatenate(
        [got[:, ROWS * m : ROWS * m + share].T for m in range(cols)], axis=1
    )
    total = call(functools.partial(total_kernel, layers), "total", shape, (got,))
    full = exchange(total.reshape(plane, layers, 128), PLANE).reshape(n, 128)
    stem_grad, gain_grad = call(
        functools.partial(finish_kernel, layers),
        "finish",
        (
            jax.ShapeDtypeStruct((TAPS, channels), F32),
            jax.ShapeDtypeStruct((channels,), F32),
        ),
        (full,),
    )
    return (conv_grad, stem_grad, gain_grad)


def solution(mesh):
    seq, win = mesh.devices.shape
    layers = LAYERS if seq % LAYERS == 0 else 1
    mesh = Mesh(mesh.devices.reshape(layers, seq // layers, win), AXES)
    line = ("layer", "row")
    in_specs = (P("win", line), P(), P(), P(AXES, None), P("win", line, None))
    out_specs = (P(AXES, None), P(), P())
    return jax.shard_map(shards, mesh=mesh, in_specs=in_specs, out_specs=out_specs, check_vma=False)
```

```python
import functools

import jax
import jax.numpy as jnp
from jax import lax
from jax.experimental import pallas as pl
from jax.experimental.pallas import tpu as pltpu
from jax.sharding import Mesh, PartitionSpec as P

KW = 5
TAPS = 4 * KW
PLANE = ("row", "win")
AXES = ("layer",) + PLANE
F32 = jnp.float32
BF16 = jnp.bfloat16
HIGH = lax.Precision.HIGHEST
ROOT = 0.7978845608028654
CUBE = 0.044715
ROWS, SUMS, LINE = 16, TAPS + 1, 6
CELLS = 4
LAG = 1
LAYERS = 8
NN, NT = (((1,), (0,)), ((), ())), (((1,), (1,)), ((), ()))


def pieces(x, count):
    out = []
    for _ in range(count):
        top = x.astype(BF16)
        out.append(top)
        x = x - top.astype(F32)
    return out


def dot(a, b, dims, precision=None):
    return lax.dot_general(a, b, dims, precision=precision, preferred_element_type=F32)


def twice_gelu_slope(x):
    sq = x * x
    th = jnp.tanh(x * (ROOT + (ROOT * CUBE) * sq))
    return (1.0 + th) * (1.0 + (1.0 - th) * (x * (ROOT + (3.0 * ROOT * CUBE) * sq)))


def pack_kernel(n, bases_hbm, weight_hbm, cot_hbm, out_ref, bases_ref, weight_ref, cot_ref, hold, sems):
    copies = [
        pltpu.make_async_copy(*pair, sems.at[i])
        for i, pair in enumerate(
            ((cot_hbm, cot_ref), (weight_hbm, weight_ref), (bases_hbm, bases_ref))
        )
    ]
    for copy in copies:
        copy.start()
    for copy in copies:
        copy.wait()
    half = cot_ref.shape[0]
    share, channels = weight_ref.shape
    cols = channels // n
    for m in range(cols):
        hold[pl.ds(m, n, stride=LINE), :] = cot_ref[:, m * n : (m + 1) * n].astype(F32).T
    count = 2 * half
    place = lax.broadcasted_iota(jnp.int32, (count, count), 0)
    lane = lax.broadcasted_iota(jnp.int32, (count, count), 1)
    wanted = jnp.where(lane < half, 2 * lane, 2 * (lane - half) + 1)
    pick = (place == wanted).astype(BF16)
    row = bases_ref[...].astype(F32).astype(BF16)
    split = dot(jnp.broadcast_to(row, (8, count)), pick, NN)
    hold[pl.ds(3, n, stride=LINE), :] = jnp.broadcast_to(split[0:1, :half], (n, half))
    hold[pl.ds(4, n, stride=LINE), :] = jnp.broadcast_to(split[0:1, half:], (n, half))
    weight = weight_ref[...].astype(F32)
    rows = []
    for m in range(cols):
        rows += [weight[:, m * n : (m + 1) * n], jnp.zeros((ROWS - share, n), F32)]
    rows.append(jnp.zeros((half - cols * ROWS, n), F32))
    hold[pl.ds(5, n, stride=LINE), :] = jnp.concatenate(rows, axis=0).T
    out_ref[...] = hold[...].astype(BF16)


def main_kernel(
    layers, seq, win, me_ref, got_ref, stem_ref, gain_ref, gained_ref, gram_ref, chosen_ref, turn_ref, out_ref, hold, symbols
):
    n = seq * win
    plane = n // layers
    channels = stem_ref.shape[1]
    cols = channels // n
    hold[: LINE * n, :] = got_ref[...].astype(F32)
    hold[LINE * n :, :] = jnp.zeros((8, 128), F32)
    chosen = chosen_ref[...]
    turn = turn_ref[...]

    own = hold[pl.ds(5, n, stride=LINE), :].T[: ROWS * cols].astype(BF16)
    share, block = KW * channels // n, min(256, channels)
    spread = []
    for at in range(0, KW * channels, block):
        low, high = at // share // 128 * 128, ((at + block - 1) // share // 128 + 1) * 128
        spread.append(dot(own[:, low:high], chosen[low:high, at : at + block], NN))
    spread = jnp.concatenate(spread, axis=1)
    line = [
        jnp.sum(spread[ROWS * m : ROWS * (m + 1)] * turn, axis=0, keepdims=True)
        for m in range(cols)
    ]
    line = jnp.concatenate(line + [jnp.zeros_like(line[0])] * (4 - cols), axis=0)
    weights = jnp.concatenate(
        [line[:, t * channels : (t + 1) * channels] for t in range(KW)], axis=0
    ).astype(BF16)
    mixed = dot(weights, gained_ref[...], NT)
    mixed = mixed[:, 0:TAPS] + mixed[:, 24 : 24 + TAPS] + mixed[:, 48 : 48 + TAPS]
    blank = jnp.zeros((4, 4), F32)
    table = []
    for t in range(KW):
        tap = mixed[4 * t : 4 * t + 4]
        pair = [jnp.concatenate([tap, blank], axis=1), jnp.concatenate([blank, tap], axis=1)]
        table += pair if t % 2 == 0 else pair[::-1]
    table = [part.astype(F32) for part in pieces(jnp.concatenate(table, axis=0), 3)]
    table = jnp.concatenate([jnp.concatenate(table, axis=1), jnp.zeros((32, 72), F32)], axis=0)
    table = (table + gram_ref[...]).astype(BF16)

    width = 128 * CELLS
    count = seq // CELLS
    sub = lax.broadcasted_iota(jnp.int32, (8, 128), 0)
    lane = lax.broadcasted_iota(jnp.int32, (8, 128), 1)
    wide = lax.broadcasted_iota(jnp.int32, (8, width), 0)
    top = wide < 4
    first, last = lane == 0, lane == 127
    base = (wide % 4).astype(F32)
    spare, early, low = wide % 4 == 3, wide % 2 == 0, wide % 4 < 2

    def swap(x):
        return pltpu.roll(x, 4, 0)

    def quad_sum(x):
        x = x + jnp.where(early, pltpu.roll(x, 7, 0), pltpu.roll(x, 1, 0))
        return x + jnp.where(low, pltpu.roll(x, 6, 0), pltpu.roll(x, 2, 0))

    def turn_cells(x, by):
        return [pltpu.roll(x[:, 128 * i : 128 * i + 128], by, 1) for i in range(CELLS)]

    def down(prior, turned):
        shifted = [0.0 if prior is None else prior[-1]] + turned[:-1]
        return jnp.concatenate([jnp.where(first, a, b) for a, b in zip(shifted, turned)], axis=1)

    def up(later, turned):
        shifted = turned[1:] + [0.0 if later is None else later[0]]
        return jnp.concatenate([jnp.where(last, a, b) for a, b in zip(shifted, turned)], axis=1)

    side = lax.broadcasted_iota(jnp.int32, (win, 128), 1)
    for parity in range(2):
        own = hold[pl.ds(3 + parity, n, stride=LINE), :]
        own = [own[win * s : win * s + win] for s in range(seq)]
        behind = [-1.0] + [pltpu.roll(x, 1, 1) for x in own]
        ahead = [pltpu.roll(x, 127, 1) for x in own] + [-1.0]
        for s in range(seq):
            symbols[parity, pl.ds(win * s, win), :] = jnp.where(side == 0, behind[s], behind[s + 1])
            symbols[2 + parity, pl.ds(win * s, win), :] = own[s]
            symbols[4 + parity, pl.ds(win * s, win), :] = jnp.where(side == 127, ahead[s + 1], ahead[s])

    def load(w, c):
        dr, hots = [], [[], [], []]
        for s in range(c * CELLS, (c + 1) * CELLS):
            at = s * win + w
            cell = jnp.where(sub < cols, 0.25 * hold[LINE * at : LINE * at + 8, :], 0.0)
            dr.append(cell + pltpu.roll(cell, 4, 0))
            for i in range(3):
                pair = [
                    jnp.broadcast_to(symbols[2 * i + parity, pl.ds(at, 1), :], (8, 128))
                    for parity in range(2)
                ]
                hots[i].append(jnp.where(sub < 4, *pair))
        hots = [(jnp.concatenate(x, axis=1) == base).astype(F32) for x in hots]
        return jnp.concatenate(dr, axis=1), jnp.concatenate(hots, axis=0)

    def look(cell):
        dr, hots = cell
        narrow = hots.astype(BF16)
        looked = dot(table, jnp.concatenate([narrow] * 3, axis=0), NN)
        taps = [looked[8 * t : 8 * t + 8] for t in range(KW)]
        mean_e = looked[40:48] * hots[0:8] + looked[48:56] * hots[8:16]
        mean_o = looked[56:64] * hots[8:16] + looked[64:72] * hots[16:24]
        mean = jnp.where(top, mean_e, mean_o) + swap(jnp.where(top, mean_o, mean_e))
        scale = lax.rsqrt(quad_sum(mean + jnp.where(spare, taps[0], 0.0)) + 1e-06)
        swapped = swap(scale)
        p0, p2, p4 = taps[0] * scale, taps[2] * scale, taps[4] * scale
        p1, p3 = taps[1] * swapped, taps[3] * swapped
        behind = turn_cells(p0 + jnp.where(top, p1, 0.0), 1)
        ahead = turn_cells(p4 + jnp.where(top, 0.0, p3), 127)
        return (p2 + jnp.where(top, p3, p1), ahead, behind), (
            hots, narrow, taps, scale, swapped, dr
        )

    def slope(prior, cell, later, dr):
        pre = cell[0] + down(prior and prior[2], cell[2]) + up(later and later[1], cell[1])
        dpre = dr * twice_gelu_slope(pre)
        return dpre, turn_cells(dpre, 127), turn_cells(dpre, 1)

    def close(prior, cell, later, kept):
        hots, narrow, taps, scale, swapped, dr = kept
        dpre = cell[0]
        ahead = up(later and later[1], cell[1])
        behind = down(prior and prior[2], cell[2])
        d1 = jnp.where(top, ahead, dpre)
        d3 = jnp.where(top, dpre, behind)
        here = taps[0] * ahead + taps[2] * dpre + taps[4] * behind
        there = taps[1] * d1 + taps[3] * d3
        bend = quad_sum(here + swap(there)) * (scale * scale * scale)
        other = swap(bend)
        lead = jnp.where(spare, bend, ahead * scale)
        rows = [lead, d1 * swapped, dpre * scale, d3 * swapped, behind * scale, dr]
        rows = jnp.concatenate(rows, axis=0).astype(BF16)
        even, odd = jnp.where(top, bend, other), jnp.where(top, other, bend)
        even = jnp.concatenate([even, even], axis=0).astype(BF16) * narrow[0:16]
        odd = jnp.concatenate([odd, odd], axis=0).astype(BF16) * hots[8:24].astype(BF16)
        return dot(jnp.concatenate([rows, even, odd], axis=0), narrow, NT)

    total = jnp.zeros((80, 24), F32)
    jobs = []
    for w in range(win):
        jobs += [(w, c) for c in range(count)]
    looked, kept, slopes = {}, {}, {}
    for step in range(len(jobs) + LAG + LAG):
        if step < len(jobs):
            job = jobs[step]
            looked[job], kept[job] = look(load(*job))
        if 0 <= step - LAG < len(jobs):
            w, c = jobs[step - LAG]
            slopes[w, c] = slope(
                looked.get((w, c - 1)), looked[w, c], looked.get((w, c + 1)), kept[w, c][5]
            )
        if 0 <= step - LAG - LAG < len(jobs):
            w, c = jobs[step - LAG - LAG]
            total = total + close(
                slopes.get((w, c - 1)), slopes[w, c], slopes.get((w, c + 1)), kept[w, c]
            )

    stem = stem_ref[...]
    gain = gain_ref[...]
    sums = []
    for t in range(KW + 1):
        cell = total[8 * t : 8 * t + 8]
        even, odd = (cell[0:4], cell[4:8]) if t % 2 == 0 or t == KW else (cell[4:8], cell[0:4])
        sums.append(even[:, :TAPS] + odd[:, 4:])
    grads = jnp.concatenate(sums[:KW], axis=0)
    even, odd = total[48:64, :TAPS], total[64:80, 4:]
    same = lax.broadcasted_iota(jnp.int32, (4, 4), 0) == lax.broadcasted_iota(jnp.int32, (4, 4), 1)
    even_end = [even[:, 16:].T, jnp.where(same, total[3:4, 16:TAPS], 0.0)]
    odd_end = [jnp.where(same, total[7:8, 4:8], 0.0), odd[:, :4].T]
    crossed = jnp.concatenate([even, jnp.concatenate(even_end, axis=1)], axis=0)
    crossed = crossed + jnp.concatenate([jnp.concatenate(odd_end, axis=1), odd], axis=0)
    conv = dot(grads, stem * gain, NN, HIGH)
    conv = jnp.concatenate([conv[4 * t : 4 * t + 4] for t in range(KW)], axis=1)
    conv = jnp.concatenate([conv[m : m + 1] * turn for m in range(cols)], axis=0)
    conv = jnp.concatenate(pieces(conv, 2), axis=0)
    turned = [jnp.zeros((min(16, n), 2 * ROWS * cols), F32)] * max(1, n // 16)
    for at in range(0, KW * channels, block):
        low, high = at // share // 16, (at + block - 1) // share // 16 + 1
        part = dot(chosen[16 * low : 16 * high, at : at + block], conv[:, at : at + block], NT)
        for i in range(low, high):
            turned[i] = turned[i] + part[16 * (i - low) : 16 * (i - low + 1)]
    turned = jnp.concatenate(turned, axis=0)
    turned = turned[:, : ROWS * cols] + turned[:, ROWS * cols :]
    back = jnp.zeros((TAPS, channels), F32)
    for part in pieces(grads.T, 3):
        back = back + dot(part, weights, NN)
    stem_part = gain * back - dot(crossed * (1.0 / channels), stem, NN, HIGH)
    gain_part = jnp.sum(stem * back, axis=0, keepdims=True)
    small = jnp.concatenate([stem_part, gain_part], axis=0)
    direct = jnp.concatenate([2.0 * sums[KW].T, jnp.zeros((1, 4), F32)], axis=0)
    mine = lax.broadcasted_iota(jnp.int32, (SUMS, n), 1) == me_ref[0]
    rows = []
    for m in range(cols):
        rows.append(small[:, m * n : (m + 1) * n] + jnp.where(mine, direct[:, m : m + 1], 0.0))
    rows.append(jnp.zeros((128 - cols * (ROWS + SUMS), n), F32))
    rows = jnp.concatenate([turned, jnp.concatenate(rows, axis=0).T], axis=1)
    for layer in range(layers):
        out_ref[pl.ds(layer, plane, stride=layers), :] = rows[layer * plane : (layer + 1) * plane]


def relay_kernel(layers, got_ref, out_ref):
    plane = got_ref.shape[0] // layers
    half = plane // 2
    total = got_ref[0:layers, :]
    for source in range(1, plane):
        total = total + got_ref[source * layers : (source + 1) * layers, :]
    total = [pltpu.roll(total, 48, 1), pltpu.roll(total, 16, 1)]
    total += [jnp.zeros((half - 2 * layers, 128), F32)] if half > 2 * layers else []
    total = jnp.concatenate(total, axis=0)
    lane = lax.broadcasted_iota(jnp.int32, total.shape, 1)
    for layer in range(layers):
        rows = got_ref[pl.ds(layer, plane, stride=layers), :]
        pair = jnp.where(lane < 48, rows[:half], pltpu.roll(rows[half:], 48, 1))
        out_ref[layer * half : (layer + 1) * half, :] = jnp.where(lane < 96, pair, total)


def total_kernel(layers, plane, got_ref, out_ref):
    half = plane // 2
    parts = []
    for at in (0, layers):
        part = got_ref[at : at + layers, :]
        for layer in range(1, layers):
            part = part + got_ref[layer * half + at : layer * half + at + layers, :]
        parts.append(part)
    lane = lax.broadcasted_iota(jnp.int32, parts[0].shape, 1)
    total = jnp.where(lane < 32, pltpu.roll(parts[0], 32, 1), pltpu.roll(parts[1], 64, 1))
    for target in range(plane):
        out_ref[target * layers : (target + 1) * layers, :] = total


def finish_kernel(layers, conv_ref, small_ref, grad_ref, stem_ref, gain_ref):
    n = small_ref.shape[0]
    plane, share = n // layers, grad_ref.shape[0]
    half = plane // 2
    cols = stem_ref.shape[1] // n
    conv = []
    for layer in range(layers):
        cell = conv_ref[layer * half : (layer + 1) * half, :]
        conv += [cell, pltpu.roll(cell, 128 - 48, 1)]
    conv = jnp.concatenate(conv, axis=0).T
    small = [small_ref[pl.ds(layer, plane, stride=layers), :] for layer in range(layers)]
    small = jnp.concatenate(small, axis=0).T
    for m in range(cols):
        lanes = slice(m * n, (m + 1) * n)
        grad_ref[:, lanes] = conv[ROWS * m : ROWS * m + share]
        stem_ref[:, lanes] = small[SUMS * m : SUMS * m + TAPS]
        gain_ref[lanes] = small[SUMS * m + TAPS]


def call(kernel, name, out, operands, scratch=(), smem=0, space=pltpu.VMEM, limit=48):
    specs = [pl.BlockSpec(memory_space=pltpu.SMEM)] * smem
    specs += [pl.BlockSpec(memory_space=space)] * (len(operands) - smem)
    many = isinstance(out, tuple)
    spec = pl.BlockSpec(memory_space=pltpu.VMEM)
    return pl.pallas_call(
        kernel,
        name=name,
        out_shape=out,
        in_specs=specs,
        out_specs=(spec,) * len(out) if many else spec,
        scratch_shapes=list(scratch),
        compiler_params=pltpu.CompilerParams(vmem_limit_bytes=limit * 1024 * 1024),
    )(*operands)


def exchange(x, axes):
    return lax.all_to_all(x, axes, 0, 0, tiled=True)


def shards(bases, stem_weight, norm_gain, conv_weight, cotangent):
    layers, win = lax.axis_size("layer"), lax.axis_size("win")
    seq = layers * lax.axis_size("row")
    n = seq * win
    plane = n // layers
    channels = norm_gain.shape[0]
    cols = channels // n
    half = bases.shape[1] // 2
    share = conv_weight.shape[0]
    me = lax.axis_index(AXES)

    sent = call(
        functools.partial(pack_kernel, n),
        "pack",
        jax.ShapeDtypeStruct((LINE * n, half), BF16),
        (bases, conv_weight, cotangent[0]),
        [
            pltpu.VMEM(bases.shape, jnp.int32),
            pltpu.VMEM(conv_weight.shape, BF16),
            pltpu.VMEM(cotangent.shape[1:], BF16),
            pltpu.VMEM((LINE * n, half), F32),
            pltpu.SemaphoreType.DMA((3,)),
        ],
        space=pltpu.HBM,
        limit=60,
    )
    got = exchange(sent.reshape(n, LINE // 2, 2, half), AXES).reshape(LINE * n, half)

    gained = stem_weight * norm_gain
    gained = [jnp.pad(part, ((0, 4), (0, 0))) for part in pieces(gained, 3)]
    gained = jnp.concatenate(gained, axis=0)
    gram = jnp.dot(stem_weight, stem_weight.T, precision=HIGH) * (1.0 / channels)
    tap = jnp.arange(TAPS) // 4
    ahead, same = tap[None] > tap[:, None], tap[None] == tap[:, None]
    even = jnp.pad(gram * (2.0 * ahead + same), ((0, 0), (0, 4)))
    odd = jnp.pad(gram * (2.0 * ahead.T + same), ((0, 0), (4, 0)))
    ends = jnp.diag(gram)
    lines = jnp.arange(8 * KW)[:, None]
    ends = jnp.where(lines == 3, jnp.pad(ends, (0, 4)) * (jnp.arange(24) >= 16), 0.0) + jnp.where(
        lines == 7, jnp.pad(ends, (4, 0)) * (jnp.arange(24) < 8), 0.0
    )
    gram = jnp.concatenate([ends, even[:16], odd[4:]], axis=0)
    gram = jnp.concatenate([part.astype(F32) for part in pieces(gram, 3)], axis=1)
    row = jnp.arange(KW * channels, dtype=jnp.int32)[None, :]
    chosen = (row // share == jnp.arange(n, dtype=jnp.int32)[:, None]).astype(BF16)
    turn = (row % share == jnp.arange(ROWS, dtype=jnp.int32)[:, None]).astype(F32)

    packed = call(
        functools.partial(main_kernel, layers, seq, win),
        "main",
        jax.ShapeDtypeStruct((n, 128), F32),
        (me.reshape(1), got, stem_weight, norm_gain[None], gained, gram, chosen, turn),
        [pltpu.VMEM((LINE * n + 8, 128), F32), pltpu.VMEM((6, n, 128), F32)],
        1,
    )
    got = exchange(packed.reshape(plane, layers, 128), PLANE).reshape(n, 128)
    relayed = call(
        functools.partial(relay_kernel, layers),
        "relay",
        jax.ShapeDtypeStruct((n // 2, 128), F32),
        (got,),
    )
    conv = exchange(relayed.reshape(layers, plane // 2, 128), "layer").reshape(n // 2, 128)
    total = call(
        functools.partial(total_kernel, layers, plane),
        "total",
        jax.ShapeDtypeStruct((n, 128), F32),
        (conv,),
    )
    small = exchange(total.reshape(plane, layers, 128), PLANE).reshape(n, 128)
    return call(
        functools.partial(finish_kernel, layers),
        "finish",
        (
            jax.ShapeDtypeStruct((share, channels), F32),
            jax.ShapeDtypeStruct((TAPS, channels), F32),
            jax.ShapeDtypeStruct((channels,), F32),
        ),
        (conv, small),
    )


def solution(mesh):
    seq, win = mesh.devices.shape
    layers = LAYERS if seq % LAYERS == 0 else 1
    mesh = Mesh(mesh.devices.reshape(layers, seq // layers, win), AXES)
    line = ("layer", "row")
    in_specs = (P("win", line), P(), P(), P(AXES, None), P("win", line, None))
    out_specs = (P(AXES, None), P(), P())
    return jax.shard_map(shards, mesh=mesh, in_specs=in_specs, out_specs=out_specs, check_vma=False)
```

```python
import functools

import jax
import jax.numpy as jnp
from jax import lax
from jax.experimental import pallas as pl
from jax.experimental.pallas import tpu as pltpu
from jax.sharding import Mesh, PartitionSpec as P

KW = 5
TAPS = 4 * KW
PLANE = ("row", "win")
AXES = ("layer",) + PLANE
F32 = jnp.float32
BF16 = jnp.bfloat16
HIGH = lax.Precision.HIGHEST
ROOT = 0.7978845608028654
CUBE = 0.044715
ROWS, SUMS, LINE = 16, TAPS + 1, 6
CELLS = 4
LAG = 1
LAYERS = 8
NN, NT = (((1,), (0,)), ((), ())), (((1,), (1,)), ((), ()))


def pieces(x, count):
    out = []
    for _ in range(count):
        top = x.astype(BF16)
        out.append(top)
        x = x - top.astype(F32)
    return out


def dot(a, b, dims, precision=None):
    return lax.dot_general(a, b, dims, precision=precision, preferred_element_type=F32)


def twice_gelu_slope(x):
    sq = x * x
    th = jnp.tanh(x * (ROOT + (ROOT * CUBE) * sq))
    return (1.0 + th) * (1.0 + (1.0 - th) * (x * (ROOT + (3.0 * ROOT * CUBE) * sq)))


def pack_kernel(n, bases_hbm, weight_hbm, cot_hbm, out_ref, bases_ref, weight_ref, cot_ref, hold, sems):
    copies = [
        pltpu.make_async_copy(*pair, sems.at[i])
        for i, pair in enumerate(
            ((cot_hbm, cot_ref), (weight_hbm, weight_ref), (bases_hbm, bases_ref))
        )
    ]
    for copy in copies:
        copy.start()
    for copy in copies:
        copy.wait()
    half = cot_ref.shape[0]
    share, channels = weight_ref.shape
    cols = channels // n
    for m in range(cols):
        hold[pl.ds(m, n, stride=LINE), :] = cot_ref[:, m * n : (m + 1) * n].astype(F32).T
    count = 2 * half
    place = lax.broadcasted_iota(jnp.int32, (count, count), 0)
    lane = lax.broadcasted_iota(jnp.int32, (count, count), 1)
    wanted = jnp.where(lane < half, 2 * lane, 2 * (lane - half) + 1)
    pick = (place == wanted).astype(BF16)
    row = bases_ref[...].astype(F32).astype(BF16)
    split = dot(jnp.broadcast_to(row, (8, count)), pick, NN)
    hold[pl.ds(3, n, stride=LINE), :] = jnp.broadcast_to(split[0:1, :half], (n, half))
    hold[pl.ds(4, n, stride=LINE), :] = jnp.broadcast_to(split[0:1, half:], (n, half))
    weight = weight_ref[...].astype(F32)
    rows = []
    for m in range(cols):
        rows += [weight[:, m * n : (m + 1) * n], jnp.zeros((ROWS - share, n), F32)]
    rows.append(jnp.zeros((half - cols * ROWS, n), F32))
    hold[pl.ds(5, n, stride=LINE), :] = jnp.concatenate(rows, axis=0).T
    out_ref[...] = hold[...].astype(BF16)


def main_kernel(
    layers, seq, win, me_ref, got_ref, stem_ref, gain_ref, gained_ref, gram_ref, chosen_ref, turn_ref, out_ref, hold, symbols
):
    n = seq * win
    plane = n // layers
    channels = stem_ref.shape[1]
    cols = channels // n
    hold[: LINE * n, :] = got_ref[...].astype(F32)
    hold[LINE * n :, :] = jnp.zeros((8, 128), F32)
    chosen = chosen_ref[...]
    turn = turn_ref[...]

    own = hold[pl.ds(5, n, stride=LINE), :].T[: ROWS * cols].astype(BF16)
    share, block = KW * channels // n, min(256, channels)
    spread = []
    for at in range(0, KW * channels, block):
        low, high = at // share // 128 * 128, ((at + block - 1) // share // 128 + 1) * 128
        spread.append(dot(own[:, low:high], chosen[low:high, at : at + block], NN))
    spread = jnp.concatenate(spread, axis=1)
    line = [
        jnp.sum(spread[ROWS * m : ROWS * (m + 1)] * turn, axis=0, keepdims=True)
        for m in range(cols)
    ]
    line = jnp.concatenate(line + [jnp.zeros_like(line[0])] * (4 - cols), axis=0)
    weights = jnp.concatenate(
        [line[:, t * channels : (t + 1) * channels] for t in range(KW)], axis=0
    ).astype(BF16)
    mixed = dot(weights, gained_ref[...], NT)
    mixed = mixed[:, 0:TAPS] + mixed[:, 24 : 24 + TAPS] + mixed[:, 48 : 48 + TAPS]
    blank = jnp.zeros((4, 4), F32)
    table = []
    for t in range(KW):
        tap = mixed[4 * t : 4 * t + 4]
        pair = [jnp.concatenate([tap, blank], axis=1), jnp.concatenate([blank, tap], axis=1)]
        table += pair if t % 2 == 0 else pair[::-1]
    table = [part.astype(F32) for part in pieces(jnp.concatenate(table, axis=0), 3)]
    table = jnp.concatenate([jnp.concatenate(table, axis=1), jnp.zeros((32, 72), F32)], axis=0)
    table = (table + gram_ref[...]).astype(BF16)

    width = 128 * CELLS
    count = seq // CELLS
    sub = lax.broadcasted_iota(jnp.int32, (8, 128), 0)
    lane = lax.broadcasted_iota(jnp.int32, (8, 128), 1)
    wide = lax.broadcasted_iota(jnp.int32, (8, width), 0)
    top = wide < 4
    first, last = lane == 0, lane == 127
    base = (wide % 4).astype(F32)
    spare, early, low = wide % 4 == 3, wide % 2 == 0, wide % 4 < 2

    def swap(x):
        return pltpu.roll(x, 4, 0)

    def quad_sum(x):
        x = x + jnp.where(early, pltpu.roll(x, 7, 0), pltpu.roll(x, 1, 0))
        return x + jnp.where(low, pltpu.roll(x, 6, 0), pltpu.roll(x, 2, 0))

    def turn_cells(x, by):
        return [pltpu.roll(x[:, 128 * i : 128 * i + 128], by, 1) for i in range(CELLS)]

    def down(prior, turned):
        shifted = [0.0 if prior is None else prior[-1]] + turned[:-1]
        return jnp.concatenate([jnp.where(first, a, b) for a, b in zip(shifted, turned)], axis=1)

    def up(later, turned):
        shifted = turned[1:] + [0.0 if later is None else later[0]]
        return jnp.concatenate([jnp.where(last, a, b) for a, b in zip(shifted, turned)], axis=1)

    side = lax.broadcasted_iota(jnp.int32, (win, 128), 1)
    for parity in range(2):
        own = hold[pl.ds(3 + parity, n, stride=LINE), :]
        own = [own[win * s : win * s + win] for s in range(seq)]
        behind = [-1.0] + [pltpu.roll(x, 1, 1) for x in own]
        ahead = [pltpu.roll(x, 127, 1) for x in own] + [-1.0]
        for s in range(seq):
            symbols[parity, pl.ds(win * s, win), :] = jnp.where(side == 0, behind[s], behind[s + 1])
            symbols[2 + parity, pl.ds(win * s, win), :] = own[s]
            symbols[4 + parity, pl.ds(win * s, win), :] = jnp.where(side == 127, ahead[s + 1], ahead[s])

    def load(w, c):
        dr, hots = [], [[], [], []]
        for s in range(c * CELLS, (c + 1) * CELLS):
            at = s * win + w
            cell = jnp.where(sub < cols, hold[LINE * at : LINE * at + 8, :], 0.0)
            dr.append(cell + pltpu.roll(cell, 4, 0))
            for i in range(3):
                pair = [
                    jnp.broadcast_to(symbols[2 * i + parity, pl.ds(at, 1), :], (8, 128))
                    for parity in range(2)
                ]
                hots[i].append(jnp.where(sub < 4, *pair))
        hots = [jnp.maximum(1.0 - jnp.abs(jnp.concatenate(x, axis=1) - base), 0.0) for x in hots]
        return jnp.concatenate(dr, axis=1), jnp.concatenate(hots, axis=0)

    def look(cell):
        dr, hots = cell
        narrow = hots.astype(BF16)
        looked = dot(table, jnp.concatenate([narrow] * 3, axis=0), NN)
        taps = [looked[8 * t : 8 * t + 8] for t in range(KW)]
        mean_e = looked[40:48] * hots[0:8] + looked[48:56] * hots[8:16]
        mean_o = looked[56:64] * hots[8:16] + looked[64:72] * hots[16:24]
        mean = jnp.where(top, mean_e, mean_o) + swap(jnp.where(top, mean_o, mean_e))
        mean = quad_sum(mean + jnp.where(spare, taps[0], 0.0))
        scale = lax.rsqrt(jnp.maximum(mean, 0.0) + 1e-06)
        swapped = swap(scale)
        p0, p2, p4 = taps[0] * scale, taps[2] * scale, taps[4] * scale
        p1, p3 = taps[1] * swapped, taps[3] * swapped
        behind = turn_cells(p0 + jnp.where(top, p1, 0.0), 1)
        ahead = turn_cells(p4 + jnp.where(top, 0.0, p3), 127)
        return (p2 + jnp.where(top, p3, p1), ahead, behind), (
            hots, narrow, taps, scale, swapped, dr
        )

    def slope(prior, cell, later, dr):
        pre = cell[0] + down(prior and prior[2], cell[2]) + up(later and later[1], cell[1])
        dpre = dr * twice_gelu_slope(pre)
        return dpre, turn_cells(dpre, 127), turn_cells(dpre, 1)

    def close(prior, cell, later, kept):
        hots, narrow, taps, scale, swapped, dr = kept
        dpre = cell[0]
        ahead = up(later and later[1], cell[1])
        behind = down(prior and prior[2], cell[2])
        d1 = jnp.where(top, ahead, dpre)
        d3 = jnp.where(top, dpre, behind)
        here = taps[0] * ahead + taps[2] * dpre + taps[4] * behind
        there = taps[1] * d1 + taps[3] * d3
        bend = here + swap(there)
        bend = pltpu.roll(bend, 1, 0) + pltpu.roll(bend, 2, 0) + pltpu.roll(bend, 3, 0)
        bend = bend * (scale * scale * scale)
        lead = jnp.where(spare, bend, ahead * scale)
        rows = [lead, d1 * swapped, dpre * scale, d3 * swapped, behind * scale, dr]
        even = jnp.broadcast_to(bend[3:4], bend.shape)
        odd = jnp.broadcast_to(bend[7:8], bend.shape)
        rows += [even * hots[0:8], even * hots[8:16], odd * hots[8:16], odd * hots[16:24]]
        return dot(jnp.concatenate(rows, axis=0), hots, NT)

    total = jnp.zeros((80, 24), F32)
    jobs = []
    for w in range(win):
        jobs += [(w, c) for c in range(count)]
    looked, kept, slopes = {}, {}, {}
    for step in range(len(jobs) + LAG + LAG):
        if step < len(jobs):
            job = jobs[step]
            looked[job], kept[job] = look(load(*job))
        if 0 <= step - LAG < len(jobs):
            w, c = jobs[step - LAG]
            slopes[w, c] = slope(
                looked.get((w, c - 1)), looked[w, c], looked.get((w, c + 1)), kept[w, c][5]
            )
        if 0 <= step - LAG - LAG < len(jobs):
            w, c = jobs[step - LAG - LAG]
            total = total + close(
                slopes.get((w, c - 1)), slopes[w, c], slopes.get((w, c + 1)), kept[w, c]
            )

    stem = stem_ref[...]
    gain = gain_ref[...]
    total = 0.25 * total
    sums = []
    for t in range(KW + 1):
        cell = total[8 * t : 8 * t + 8]
        even, odd = (cell[0:4], cell[4:8]) if t % 2 == 0 or t == KW else (cell[4:8], cell[0:4])
        sums.append(even[:, :TAPS] + odd[:, 4:])
    grads = jnp.concatenate(sums[:KW], axis=0)
    even, odd = total[48:64, :TAPS], total[64:80, 4:]
    same = lax.broadcasted_iota(jnp.int32, (4, 4), 0) == lax.broadcasted_iota(jnp.int32, (4, 4), 1)
    even_end = [even[:, 16:].T, jnp.where(same, total[3:4, 16:TAPS], 0.0)]
    odd_end = [jnp.where(same, total[7:8, 4:8], 0.0), odd[:, :4].T]
    crossed = jnp.concatenate([even, jnp.concatenate(even_end, axis=1)], axis=0)
    crossed = crossed + jnp.concatenate([jnp.concatenate(odd_end, axis=1), odd], axis=0)
    conv = dot(grads, stem * gain, NN, HIGH)
    conv = jnp.concatenate([conv[4 * t : 4 * t + 4] for t in range(KW)], axis=1)
    conv = jnp.concatenate([conv[m : m + 1] * turn for m in range(cols)], axis=0)
    conv = jnp.concatenate(pieces(conv, 2), axis=0)
    turned = [jnp.zeros((min(16, n), 2 * ROWS * cols), F32)] * max(1, n // 16)
    for at in range(0, KW * channels, block):
        low, high = at // share // 16, (at + block - 1) // share // 16 + 1
        part = dot(chosen[16 * low : 16 * high, at : at + block], conv[:, at : at + block], NT)
        for i in range(low, high):
            turned[i] = turned[i] + part[16 * (i - low) : 16 * (i - low + 1)]
    turned = jnp.concatenate(turned, axis=0)
    turned = turned[:, : ROWS * cols] + turned[:, ROWS * cols :]
    back = jnp.zeros((TAPS, channels), F32)
    for part in pieces(grads.T, 3):
        back = back + dot(part, weights, NN)
    stem_part = gain * back - dot(crossed * (1.0 / channels), stem, NN, HIGH)
    gain_part = jnp.sum(stem * back, axis=0, keepdims=True)
    small = jnp.concatenate([stem_part, gain_part], axis=0)
    direct = jnp.concatenate([2.0 * sums[KW].T, jnp.zeros((1, 4), F32)], axis=0)
    mine = lax.broadcasted_iota(jnp.int32, (SUMS, n), 1) == me_ref[0]
    rows = []
    for m in range(cols):
        rows.append(small[:, m * n : (m + 1) * n] + jnp.where(mine, direct[:, m : m + 1], 0.0))
    rows.append(jnp.zeros((128 - cols * (ROWS + SUMS), n), F32))
    rows = jnp.concatenate([turned, jnp.concatenate(rows, axis=0).T], axis=1)
    for layer in range(layers):
        out_ref[pl.ds(layer, plane, stride=layers), :] = rows[layer * plane : (layer + 1) * plane]


def relay_kernel(layers, got_ref, out_ref):
    plane = got_ref.shape[0] // layers
    half = plane // 2
    total = got_ref[0:layers, :]
    for source in range(1, plane):
        total = total + got_ref[source * layers : (source + 1) * layers, :]
    total = [pltpu.roll(total, 48, 1), pltpu.roll(total, 16, 1)]
    total += [jnp.zeros((half - 2 * layers, 128), F32)] if half > 2 * layers else []
    total = jnp.concatenate(total, axis=0)
    lane = lax.broadcasted_iota(jnp.int32, total.shape, 1)
    for layer in range(layers):
        rows = got_ref[pl.ds(layer, plane, stride=layers), :]
        pair = jnp.where(lane < 48, rows[:half], pltpu.roll(rows[half:], 48, 1))
        out_ref[layer * half : (layer + 1) * half, :] = jnp.where(lane < 96, pair, total)


def total_kernel(layers, plane, got_ref, out_ref):
    half = plane // 2
    parts = []
    for at in (0, layers):
        part = got_ref[at : at + layers, :]
        for layer in range(1, layers):
            part = part + got_ref[layer * half + at : layer * half + at + layers, :]
        parts.append(part)
    lane = lax.broadcasted_iota(jnp.int32, parts[0].shape, 1)
    total = jnp.where(lane < 32, pltpu.roll(parts[0], 32, 1), pltpu.roll(parts[1], 64, 1))
    for target in range(plane):
        out_ref[target * layers : (target + 1) * layers, :] = total


def finish_kernel(layers, conv_ref, small_ref, grad_ref, stem_ref, gain_ref):
    n = small_ref.shape[0]
    plane, share = n // layers, grad_ref.shape[0]
    half = plane // 2
    cols = stem_ref.shape[1] // n
    conv = []
    for layer in range(layers):
        cell = conv_ref[layer * half : (layer + 1) * half, :]
        conv += [cell, pltpu.roll(cell, 128 - 48, 1)]
    conv = jnp.concatenate(conv, axis=0).T
    small = [small_ref[pl.ds(layer, plane, stride=layers), :] for layer in range(layers)]
    small = jnp.concatenate(small, axis=0).T
    for m in range(cols):
        lanes = slice(m * n, (m + 1) * n)
        grad_ref[:, lanes] = conv[ROWS * m : ROWS * m + share]
        stem_ref[:, lanes] = small[SUMS * m : SUMS * m + TAPS]
        gain_ref[lanes] = small[SUMS * m + TAPS]


def call(kernel, name, out, operands, scratch=(), smem=0, space=pltpu.VMEM, limit=48):
    specs = [pl.BlockSpec(memory_space=pltpu.SMEM)] * smem
    specs += [pl.BlockSpec(memory_space=space)] * (len(operands) - smem)
    many = isinstance(out, tuple)
    spec = pl.BlockSpec(memory_space=pltpu.VMEM)
    return pl.pallas_call(
        kernel,
        name=name,
        out_shape=out,
        in_specs=specs,
        out_specs=(spec,) * len(out) if many else spec,
        scratch_shapes=list(scratch),
        compiler_params=pltpu.CompilerParams(vmem_limit_bytes=limit * 1024 * 1024),
    )(*operands)


def exchange(x, axes):
    return lax.all_to_all(x, axes, 0, 0, tiled=True)


def shards(bases, stem_weight, norm_gain, conv_weight, cotangent):
    layers, win = lax.axis_size("layer"), lax.axis_size("win")
    seq = layers * lax.axis_size("row")
    n = seq * win
    plane = n // layers
    channels = norm_gain.shape[0]
    cols = channels // n
    half = bases.shape[1] // 2
    share = conv_weight.shape[0]
    me = lax.axis_index(AXES)

    sent = call(
        functools.partial(pack_kernel, n),
        "pack",
        jax.ShapeDtypeStruct((LINE * n, half), BF16),
        (bases, conv_weight, cotangent[0]),
        [
            pltpu.VMEM(bases.shape, jnp.int32),
            pltpu.VMEM(conv_weight.shape, BF16),
            pltpu.VMEM(cotangent.shape[1:], BF16),
            pltpu.VMEM((LINE * n, half), F32),
            pltpu.SemaphoreType.DMA((3,)),
        ],
        space=pltpu.HBM,
        limit=60,
    )
    got = exchange(sent.reshape(n, LINE // 2, 2, half), AXES).reshape(LINE * n, half)

    gained = stem_weight * norm_gain
    gained = [jnp.pad(part, ((0, 4), (0, 0))) for part in pieces(gained, 3)]
    gained = jnp.concatenate(gained, axis=0)
    gram = jnp.dot(stem_weight, stem_weight.T, precision=HIGH) * (1.0 / channels)
    tap = jnp.arange(TAPS) // 4
    ahead, same = tap[None] > tap[:, None], tap[None] == tap[:, None]
    even = jnp.pad(gram * (2.0 * ahead + same), ((0, 0), (0, 4)))
    odd = jnp.pad(gram * (2.0 * ahead.T + same), ((0, 0), (4, 0)))
    ends = jnp.diag(gram)
    lines = jnp.arange(8 * KW)[:, None]
    ends = jnp.where(lines == 3, jnp.pad(ends, (0, 4)) * (jnp.arange(24) >= 16), 0.0) + jnp.where(
        lines == 7, jnp.pad(ends, (4, 0)) * (jnp.arange(24) < 8), 0.0
    )
    gram = jnp.concatenate([ends, even[:16], odd[4:]], axis=0)
    gram = jnp.concatenate([part.astype(F32) for part in pieces(gram, 3)], axis=1)
    row = jnp.arange(KW * channels, dtype=jnp.int32)[None, :]
    chosen = (row // share == jnp.arange(n, dtype=jnp.int32)[:, None]).astype(BF16)
    turn = (row % share == jnp.arange(ROWS, dtype=jnp.int32)[:, None]).astype(F32)

    packed = call(
        functools.partial(main_kernel, layers, seq, win),
        "main",
        jax.ShapeDtypeStruct((n, 128), F32),
        (me.reshape(1), got, stem_weight, norm_gain[None], gained, gram, chosen, turn),
        [pltpu.VMEM((LINE * n + 8, 128), F32), pltpu.VMEM((6, n, 128), F32)],
        1,
    )
    got = exchange(packed.reshape(plane, layers, 128), PLANE).reshape(n, 128)
    relayed = call(
        functools.partial(relay_kernel, layers),
        "relay",
        jax.ShapeDtypeStruct((n // 2, 128), F32),
        (got,),
    )
    conv = exchange(relayed.reshape(layers, plane // 2, 128), "layer").reshape(n // 2, 128)
    total = call(
        functools.partial(total_kernel, layers, plane),
        "total",
        jax.ShapeDtypeStruct((n, 128), F32),
        (conv,),
    )
    small = exchange(total.reshape(plane, layers, 128), PLANE).reshape(n, 128)
    return call(
        functools.partial(finish_kernel, layers),
        "finish",
        (
            jax.ShapeDtypeStruct((share, channels), F32),
            jax.ShapeDtypeStruct((TAPS, channels), F32),
            jax.ShapeDtypeStruct((channels,), F32),
        ),
        (conv, small),
    )


def solution(mesh):
    seq, win = mesh.devices.shape
    layers = LAYERS if seq % LAYERS == 0 else 1
    mesh = Mesh(mesh.devices.reshape(layers, seq // layers, win), AXES)
    line = ("layer", "row")
    in_specs = (P("win", line), P(), P(), P(AXES, None), P("win", line, None))
    out_specs = (P(AXES, None), P(), P())
    return jax.shard_map(shards, mesh=mesh, in_specs=in_specs, out_specs=out_specs, check_vma=False)
```

```python
import functools

import jax
import jax.numpy as jnp
from jax import lax
from jax.experimental import pallas as pl
from jax.experimental.pallas import tpu as pltpu
from jax.sharding import Mesh, PartitionSpec as P

KW = 5
TAPS = 4 * KW
PLANE = ("row", "win")
AXES = ("layer",) + PLANE
F32 = jnp.float32
BF16 = jnp.bfloat16
HIGH = lax.Precision.HIGHEST
ROOT = 0.7978845608028654
CUBE = 0.044715
ROWS, SUMS, LINE = 16, TAPS + 1, 6
CELLS = 2
LAG = 1
LAYERS = 8
NN, NT = (((1,), (0,)), ((), ())), (((1,), (1,)), ((), ()))


def pieces(x, count):
    out = []
    for _ in range(count):
        top = x.astype(BF16)
        out.append(top)
        x = x - top.astype(F32)
    return out


def dot(a, b, dims, precision=None):
    return lax.dot_general(a, b, dims, precision=precision, preferred_element_type=F32)


def split_dot(a, b_ref):
    blank = jnp.zeros((a.shape[0], 4), F32)
    big, small = [jnp.concatenate([x.astype(F32), blank], axis=1) for x in pieces(a, 2)]
    left = jnp.concatenate([big, big, big, small, small], axis=1).astype(BF16)
    return dot(left, jnp.concatenate([b_ref[...], b_ref[:48]], axis=0), NN)


def twice_gelu_slope(x):
    sq = x * x
    th = jnp.tanh(x * (ROOT + (ROOT * CUBE) * sq))
    return (1.0 + th) * (1.0 + (1.0 - th) * (x * (ROOT + (3.0 * ROOT * CUBE) * sq)))


def pack_kernel(n, bases_hbm, weight_hbm, cot_hbm, out_ref, bases_ref, weight_ref, cot_ref, hold, sems):
    copies = [
        pltpu.make_async_copy(*pair, sems.at[i])
        for i, pair in enumerate(
            ((cot_hbm, cot_ref), (weight_hbm, weight_ref), (bases_hbm, bases_ref))
        )
    ]
    for copy in copies:
        copy.start()
    for copy in copies:
        copy.wait()
    half = cot_ref.shape[0]
    share, channels = weight_ref.shape
    cols = channels // n
    for m in range(cols):
        hold[pl.ds(m, n, stride=LINE), :] = cot_ref[:, m * n : (m + 1) * n].astype(F32).T
    count = 2 * half
    place = lax.broadcasted_iota(jnp.int32, (count, count), 0)
    lane = lax.broadcasted_iota(jnp.int32, (count, count), 1)
    wanted = jnp.where(lane < half, 2 * lane, 2 * (lane - half) + 1)
    pick = (place == wanted).astype(BF16)
    row = bases_ref[...].astype(F32).astype(BF16)
    split = dot(jnp.broadcast_to(row, (8, count)), pick, NN)
    hold[pl.ds(3, n, stride=LINE), :] = jnp.broadcast_to(split[0:1, :half], (n, half))
    hold[pl.ds(4, n, stride=LINE), :] = jnp.broadcast_to(split[0:1, half:], (n, half))
    weight = weight_ref[...].astype(F32)
    rows = []
    for m in range(cols):
        rows += [weight[:, m * n : (m + 1) * n], jnp.zeros((ROWS - share, n), F32)]
    rows.append(jnp.zeros((half - cols * ROWS, n), F32))
    hold[pl.ds(5, n, stride=LINE), :] = jnp.concatenate(rows, axis=0).T
    out_ref[...] = hold[...].astype(BF16)


def main_kernel(
    layers, seq, win, me_ref, got_ref, stem_ref, gain_ref, parts_ref, gained_ref, gram_ref, chosen_ref, turn_ref, out_ref, hold, symbols
):
    n = seq * win
    plane = n // layers
    channels = stem_ref.shape[1]
    cols = channels // n
    hold[: LINE * n, :] = got_ref[...].astype(F32)
    hold[LINE * n :, :] = jnp.zeros((8, 128), F32)
    chosen = chosen_ref[...]
    turn = turn_ref[...]

    own = hold[pl.ds(5, n, stride=LINE), :].T[: ROWS * cols].astype(BF16)
    share, block = KW * channels // n, min(256, channels)
    spread = []
    for at in range(0, KW * channels, block):
        low, high = at // share // 128 * 128, ((at + block - 1) // share // 128 + 1) * 128
        spread.append(dot(own[:, low:high], chosen[low:high, at : at + block], NN))
    spread = jnp.concatenate(spread, axis=1)
    line = [
        jnp.sum(spread[ROWS * m : ROWS * (m + 1)] * turn, axis=0, keepdims=True)
        for m in range(cols)
    ]
    line = jnp.concatenate(line + [jnp.zeros_like(line[0])] * (4 - cols), axis=0)
    weights = jnp.concatenate(
        [line[:, t * channels : (t + 1) * channels] for t in range(KW)], axis=0
    ).astype(BF16)
    mixed = dot(weights, gained_ref[...], NT)
    mixed = mixed[:, 0:TAPS] + mixed[:, 24 : 24 + TAPS] + mixed[:, 48 : 48 + TAPS]
    blank = jnp.zeros((4, 4), F32)
    table = []
    for t in range(KW):
        tap = mixed[4 * t : 4 * t + 4]
        pair = [jnp.concatenate([tap, blank], axis=1), jnp.concatenate([blank, tap], axis=1)]
        table += pair if t % 2 == 0 else pair[::-1]
    table = [part.astype(F32) for part in pieces(jnp.concatenate(table, axis=0), 3)]
    table = jnp.concatenate([jnp.concatenate(table, axis=1), gram_ref[...]], axis=0).astype(BF16)

    width = 128 * CELLS
    count = seq // CELLS
    sub = lax.broadcasted_iota(jnp.int32, (8, 128), 0)
    lane = lax.broadcasted_iota(jnp.int32, (8, 128), 1)
    wide = lax.broadcasted_iota(jnp.int32, (8, width), 0)
    top = wide < 4
    first, last = lane == 0, lane == 127
    base = (wide % 4).astype(F32)
    early, low = wide % 2 == 0, wide % 4 < 2

    def swap(x):
        return pltpu.roll(x, 4, 0)

    def quad_sum(x):
        x = x + jnp.where(early, pltpu.roll(x, 7, 0), pltpu.roll(x, 1, 0))
        return x + jnp.where(low, pltpu.roll(x, 6, 0), pltpu.roll(x, 2, 0))

    def turn_cells(x, by):
        return [pltpu.roll(x[:, 128 * i : 128 * i + 128], by, 1) for i in range(CELLS)]

    def down(prior, turned):
        shifted = [0.0 if prior is None else prior[-1]] + turned[:-1]
        return jnp.concatenate([jnp.where(first, a, b) for a, b in zip(shifted, turned)], axis=1)

    def up(later, turned):
        shifted = turned[1:] + [0.0 if later is None else later[0]]
        return jnp.concatenate([jnp.where(last, a, b) for a, b in zip(shifted, turned)], axis=1)

    side = lax.broadcasted_iota(jnp.int32, (win, 128), 1)
    for parity in range(2):
        own = hold[pl.ds(3 + parity, n, stride=LINE), :]
        own = [own[win * s : win * s + win] for s in range(seq)]
        behind = [-1.0] + [pltpu.roll(x, 1, 1) for x in own]
        ahead = [pltpu.roll(x, 127, 1) for x in own] + [-1.0]
        for s in range(seq):
            symbols[parity, pl.ds(win * s, win), :] = jnp.where(side == 0, behind[s], behind[s + 1])
            symbols[2 + parity, pl.ds(win * s, win), :] = own[s]
            symbols[4 + parity, pl.ds(win * s, win), :] = jnp.where(side == 127, ahead[s + 1], ahead[s])

    def load(w, c):
        dr, hots = [], [[], [], []]
        for s in range(c * CELLS, (c + 1) * CELLS):
            at = s * win + w
            cell = jnp.where(sub < cols, hold[LINE * at : LINE * at + 8, :], 0.0)
            dr.append(cell + pltpu.roll(cell, 4, 0))
            for i in range(3):
                pair = [
                    jnp.broadcast_to(symbols[2 * i + parity, pl.ds(at, 1), :], (8, 128))
                    for parity in range(2)
                ]
                hots[i].append(jnp.where(sub < 4, *pair))
        hots = [jnp.maximum(1.0 - jnp.abs(jnp.concatenate(x, axis=1) - base), 0.0) for x in hots]
        return jnp.concatenate(dr, axis=1), jnp.concatenate(hots, axis=0)

    def look(cell):
        dr, hots = cell
        narrow = hots.astype(BF16)
        looked = dot(table, jnp.concatenate([narrow] * 3, axis=0), NN)
        taps = [looked[8 * t : 8 * t + 8] for t in range(KW)]
        mean_e = looked[40:48] * hots[0:8] + looked[48:56] * hots[8:16]
        mean_o = looked[56:64] * hots[8:16] + looked[64:72] * hots[16:24]
        mean = jnp.where(top, mean_e, mean_o) + swap(jnp.where(top, mean_o, mean_e))
        scale = lax.rsqrt(jnp.maximum(quad_sum(mean), 0.0) + 1e-06)
        swapped = swap(scale)
        p0, p2, p4 = taps[0] * scale, taps[2] * scale, taps[4] * scale
        p1, p3 = taps[1] * swapped, taps[3] * swapped
        behind = turn_cells(p0 + jnp.where(top, p1, 0.0), 1)
        ahead = turn_cells(p4 + jnp.where(top, 0.0, p3), 127)
        return (p2 + jnp.where(top, p3, p1), ahead, behind), (
            hots, narrow, taps, scale, swapped, dr
        )

    def slope(prior, cell, later, dr):
        pre = cell[0] + down(prior and prior[2], cell[2]) + up(later and later[1], cell[1])
        dpre = dr * twice_gelu_slope(pre)
        return dpre, turn_cells(dpre, 127), turn_cells(dpre, 1)

    def close(prior, cell, later, kept):
        hots, narrow, taps, scale, swapped, dr = kept
        dpre = cell[0]
        ahead = up(later and later[1], cell[1])
        behind = down(prior and prior[2], cell[2])
        d1 = jnp.where(top, ahead, dpre)
        d3 = jnp.where(top, dpre, behind)
        here = taps[0] * ahead + taps[2] * dpre + taps[4] * behind
        there = taps[1] * d1 + taps[3] * d3
        bend = here + swap(there)
        bend = pltpu.roll(bend, 1, 0) + pltpu.roll(bend, 2, 0) + pltpu.roll(bend, 3, 0)
        bend = bend * (scale * scale * scale)
        rows = [ahead * scale, d1 * swapped, dpre * scale, d3 * swapped, behind * scale, dr]
        even = jnp.broadcast_to(bend[3:4], bend.shape)
        odd = jnp.broadcast_to(bend[7:8], bend.shape)
        rows += [even * hots[0:8], even * hots[8:16], odd * hots[8:16], odd * hots[16:24]]
        return dot(jnp.concatenate(rows, axis=0), hots, NT)

    total = jnp.zeros((80, 24), F32)
    jobs = []
    for w in range(win):
        jobs += [(w, c) for c in range(count)]
    looked, kept, slopes = {}, {}, {}
    for step in range(len(jobs) + LAG + LAG):
        if step < len(jobs):
            job = jobs[step]
            looked[job], kept[job] = look(load(*job))
        if 0 <= step - LAG < len(jobs):
            w, c = jobs[step - LAG]
            slopes[w, c] = slope(
                looked.get((w, c - 1)), looked[w, c], looked.get((w, c + 1)), kept[w, c][5]
            )
        if 0 <= step - LAG - LAG < len(jobs):
            w, c = jobs[step - LAG - LAG]
            total = total + close(
                slopes.get((w, c - 1)), slopes[w, c], slopes.get((w, c + 1)), kept[w, c]
            )

    stem = stem_ref[...]
    gain = gain_ref[...]
    total = 0.25 * total
    sums = []
    for t in range(KW + 1):
        cell = total[8 * t : 8 * t + 8]
        even, odd = (cell[0:4], cell[4:8]) if t % 2 == 0 or t == KW else (cell[4:8], cell[0:4])
        sums.append(even[:, :TAPS] + odd[:, 4:])
    grads = jnp.concatenate(sums[:KW], axis=0)
    even, odd = total[48:64, :TAPS], total[64:80, 4:]
    same = lax.broadcasted_iota(jnp.int32, (4, 4), 0) == lax.broadcasted_iota(jnp.int32, (4, 4), 1)
    even_end = [even[:, 16:].T, jnp.where(same, jnp.sum(even[12:16, 16:], axis=0, keepdims=True), 0.0)]
    odd_end = [jnp.where(same, jnp.sum(odd[0:4, :4], axis=0, keepdims=True), 0.0), odd[:, :4].T]
    crossed = jnp.concatenate([even, jnp.concatenate(even_end, axis=1)], axis=0)
    crossed = crossed + jnp.concatenate([jnp.concatenate(odd_end, axis=1), odd], axis=0)
    conv = split_dot(grads, gained_ref)
    conv = jnp.concatenate([conv[4 * t : 4 * t + 4] for t in range(KW)], axis=1)
    conv = jnp.concatenate([conv[m : m + 1] * turn for m in range(cols)], axis=0)
    conv = jnp.concatenate(pieces(conv, 2), axis=0)
    turned = [jnp.zeros((min(16, n), 2 * ROWS * cols), F32)] * max(1, n // 16)
    for at in range(0, KW * channels, block):
        low, high = at // share // 16, (at + block - 1) // share // 16 + 1
        part = dot(chosen[16 * low : 16 * high, at : at + block], conv[:, at : at + block], NT)
        for i in range(low, high):
            turned[i] = turned[i] + part[16 * (i - low) : 16 * (i - low + 1)]
    turned = jnp.concatenate(turned, axis=0)
    turned = turned[:, : ROWS * cols] + turned[:, ROWS * cols :]
    back = jnp.zeros((TAPS, channels), F32)
    for part in pieces(grads.T, 3):
        back = back + dot(part, weights, NN)
    stem_part = gain * back - split_dot(crossed * (1.0 / channels), parts_ref)
    gain_part = jnp.sum(stem * back, axis=0, keepdims=True)
    small = jnp.concatenate([stem_part, gain_part], axis=0)
    direct = jnp.concatenate([2.0 * sums[KW].T, jnp.zeros((1, 4), F32)], axis=0)
    mine = lax.broadcasted_iota(jnp.int32, (SUMS, n), 1) == me_ref[0]
    rows = []
    for m in range(cols):
        rows.append(small[:, m * n : (m + 1) * n] + jnp.where(mine, direct[:, m : m + 1], 0.0))
    rows.append(jnp.zeros((128 - cols * (ROWS + SUMS), n), F32))
    rows = jnp.concatenate([turned, jnp.concatenate(rows, axis=0).T], axis=1)
    for layer in range(layers):
        out_ref[pl.ds(layer, plane, stride=layers), :] = rows[layer * plane : (layer + 1) * plane]


def relay_kernel(layers, got_ref, out_ref):
    plane = got_ref.shape[0] // layers
    half = plane // 2
    total = got_ref[0:layers, :]
    for source in range(1, plane):
        total = total + got_ref[source * layers : (source + 1) * layers, :]
    total = [pltpu.roll(total, 48, 1), pltpu.roll(total, 16, 1)]
    total += [jnp.zeros((half - 2 * layers, 128), F32)] if half > 2 * layers else []
    total = jnp.concatenate(total, axis=0)
    lane = lax.broadcasted_iota(jnp.int32, total.shape, 1)
    for layer in range(layers):
        rows = got_ref[pl.ds(layer, plane, stride=layers), :]
        pair = jnp.where(lane < 48, rows[:half], pltpu.roll(rows[half:], 48, 1))
        out_ref[layer * half : (layer + 1) * half, :] = jnp.where(lane < 96, pair, total)


def total_kernel(layers, plane, got_ref, out_ref):
    half = plane // 2
    parts = []
    for at in (0, layers):
        part = got_ref[at : at + layers, :]
        for layer in range(1, layers):
            part = part + got_ref[layer * half + at : layer * half + at + layers, :]
        parts.append(part)
    lane = lax.broadcasted_iota(jnp.int32, parts[0].shape, 1)
    total = jnp.where(lane < 32, pltpu.roll(parts[0], 32, 1), pltpu.roll(parts[1], 64, 1))
    for target in range(plane):
        out_ref[target * layers : (target + 1) * layers, :] = total


def finish_kernel(layers, conv_ref, small_ref, grad_ref, stem_ref, gain_ref):
    n = small_ref.shape[0]
    plane, share = n // layers, grad_ref.shape[0]
    half = plane // 2
    cols = stem_ref.shape[1] // n
    conv = []
    for layer in range(layers):
        cell = conv_ref[layer * half : (layer + 1) * half, :]
        conv += [cell, pltpu.roll(cell, 128 - 48, 1)]
    conv = jnp.concatenate(conv, axis=0).T
    small = [small_ref[pl.ds(layer, plane, stride=layers), :] for layer in range(layers)]
    small = jnp.concatenate(small, axis=0).T
    for m in range(cols):
        lanes = slice(m * n, (m + 1) * n)
        grad_ref[:, lanes] = conv[ROWS * m : ROWS * m + share]
        stem_ref[:, lanes] = small[SUMS * m : SUMS * m + TAPS]
        gain_ref[lanes] = small[SUMS * m + TAPS]


def call(kernel, name, out, operands, scratch=(), smem=0, space=pltpu.VMEM, limit=48):
    specs = [pl.BlockSpec(memory_space=pltpu.SMEM)] * smem
    specs += [pl.BlockSpec(memory_space=space)] * (len(operands) - smem)
    many = isinstance(out, tuple)
    spec = pl.BlockSpec(memory_space=pltpu.VMEM)
    return pl.pallas_call(
        kernel,
        name=name,
        out_shape=out,
        in_specs=specs,
        out_specs=(spec,) * len(out) if many else spec,
        scratch_shapes=list(scratch),
        compiler_params=pltpu.CompilerParams(vmem_limit_bytes=limit * 1024 * 1024),
    )(*operands)


def exchange(x, axes):
    return lax.all_to_all(x, axes, 0, 0, tiled=True)


def shards(bases, stem_weight, norm_gain, conv_weight, cotangent):
    layers, win = lax.axis_size("layer"), lax.axis_size("win")
    seq = layers * lax.axis_size("row")
    n = seq * win
    plane = n // layers
    channels = norm_gain.shape[0]
    cols = channels // n
    half = bases.shape[1] // 2
    share = conv_weight.shape[0]
    me = lax.axis_index(AXES)

    sent = call(
        functools.partial(pack_kernel, n),
        "pack",
        jax.ShapeDtypeStruct((LINE * n, half), BF16),
        (bases, conv_weight, cotangent[0]),
        [
            pltpu.VMEM(bases.shape, jnp.int32),
            pltpu.VMEM(conv_weight.shape, BF16),
            pltpu.VMEM(cotangent.shape[1:], BF16),
            pltpu.VMEM((LINE * n, half), F32),
            pltpu.SemaphoreType.DMA((3,)),
        ],
        space=pltpu.HBM,
        limit=60,
    )
    got = exchange(sent.reshape(n, LINE // 2, 2, half), AXES).reshape(LINE * n, half)

    parts, gained = [
        jnp.concatenate([jnp.pad(part, ((0, 4), (0, 0))) for part in pieces(x, 3)], axis=0)
        for x in (stem_weight, stem_weight * norm_gain)
    ]
    gram = jnp.dot(stem_weight, stem_weight.T, precision=HIGH) * (1.0 / channels)
    tap = jnp.arange(TAPS) // 4
    ahead, same = tap[None] > tap[:, None], tap[None] == tap[:, None]
    square = jnp.diag(gram)[None]
    even = gram * (2.0 * ahead + same) + square * ((tap[:, None] == 3) & (tap[None] == 4))
    odd = gram * (2.0 * ahead.T + same) + square * ((tap[:, None] == 1) & (tap[None] == 0))
    even, odd = jnp.pad(even[:16], ((0, 0), (0, 4))), jnp.pad(odd[4:], ((0, 0), (4, 0)))
    gram = jnp.concatenate([even, odd], axis=0)
    gram = jnp.concatenate([part.astype(F32) for part in pieces(gram, 3)], axis=1)
    row = jnp.arange(KW * channels, dtype=jnp.int32)[None, :]
    chosen = (row // share == jnp.arange(n, dtype=jnp.int32)[:, None]).astype(BF16)
    turn = (row % share == jnp.arange(ROWS, dtype=jnp.int32)[:, None]).astype(F32)

    packed = call(
        functools.partial(main_kernel, layers, seq, win),
        "main",
        jax.ShapeDtypeStruct((n, 128), F32),
        (me.reshape(1), got, stem_weight, norm_gain[None], parts, gained, gram, chosen, turn),
        [pltpu.VMEM((LINE * n + 8, 128), F32), pltpu.VMEM((6, n, 128), F32)],
        1,
    )
    got = exchange(packed.reshape(plane, layers, 128), PLANE).reshape(n, 128)
    relayed = call(
        functools.partial(relay_kernel, layers),
        "relay",
        jax.ShapeDtypeStruct((n // 2, 128), F32),
        (got,),
    )
    conv = exchange(relayed.reshape(layers, plane // 2, 128), "layer").reshape(n // 2, 128)
    total = call(
        functools.partial(total_kernel, layers, plane),
        "total",
        jax.ShapeDtypeStruct((n, 128), F32),
        (conv,),
    )
    small = exchange(total.reshape(plane, layers, 128), PLANE).reshape(n, 128)
    return call(
        functools.partial(finish_kernel, layers),
        "finish",
        (
            jax.ShapeDtypeStruct((share, channels), F32),
            jax.ShapeDtypeStruct((TAPS, channels), F32),
            jax.ShapeDtypeStruct((channels,), F32),
        ),
        (conv, small),
    )


def solution(mesh):
    seq, win = mesh.devices.shape
    layers = LAYERS if seq % LAYERS == 0 else 1
    mesh = Mesh(mesh.devices.reshape(layers, seq // layers, win), AXES)
    line = ("layer", "row")
    in_specs = (P("win", line), P(), P(), P(AXES, None), P("win", line, None))
    out_specs = (P(AXES, None), P(), P())
    return jax.shard_map(shards, mesh=mesh, in_specs=in_specs, out_specs=out_specs, check_vma=False)
```

```python
import functools

import jax
import jax.numpy as jnp
from jax import lax
from jax.experimental import pallas as pl
from jax.experimental.pallas import tpu as pltpu
from jax.sharding import Mesh, PartitionSpec as P

KW = 5
TAPS = 4 * KW
PLANE = ("row", "win")
AXES = ("layer",) + PLANE
F32 = jnp.float32
BF16 = jnp.bfloat16
HIGH = lax.Precision.HIGHEST
ROOT = 0.7978845608028654
CUBE = 0.044715
ROWS, SUMS, LINE = 16, TAPS + 1, 6
CELLS = 2
LAG = 1
LAYERS = 8
NN, NT = (((1,), (0,)), ((), ())), (((1,), (1,)), ((), ()))


def pieces(x, count):
    out = []
    for _ in range(count):
        top = x.astype(BF16)
        out.append(top)
        x = x - top.astype(F32)
    return out


def outer_pieces(x, count):
    out = []
    for _ in range(count):
        top = lax.reduce_precision(x, 8, 7)
        out.append(top.astype(BF16))
        x = x - top
    return out


def dot(a, b, dims, precision=None):
    return lax.dot_general(a, b, dims, precision=precision, preferred_element_type=F32)


def split_dot(a, b_ref):
    blank = jnp.zeros((a.shape[0], 4), F32)
    big, small = [jnp.concatenate([x.astype(F32), blank], axis=1) for x in pieces(a, 2)]
    left = jnp.concatenate([big, big, big, small, small], axis=1).astype(BF16)
    return dot(left, jnp.concatenate([b_ref[...], b_ref[:48]], axis=0), NN)


def twice_gelu_slope(x):
    sq = x * x
    th = jnp.tanh(x * (ROOT + (ROOT * CUBE) * sq))
    return (1.0 + th) * (1.0 + (1.0 - th) * (x * (ROOT + (3.0 * ROOT * CUBE) * sq)))


def pack_kernel(n, bases_hbm, weight_hbm, cot_hbm, out_ref, bases_ref, weight_ref, cot_ref, hold, sems):
    copies = [
        pltpu.make_async_copy(*pair, sems.at[i])
        for i, pair in enumerate(
            ((cot_hbm, cot_ref), (weight_hbm, weight_ref), (bases_hbm, bases_ref))
        )
    ]
    for copy in copies:
        copy.start()
    for copy in copies:
        copy.wait()
    half = cot_ref.shape[0]
    share, channels = weight_ref.shape
    cols = channels // n
    for m in range(cols):
        hold[pl.ds(m, n, stride=LINE), :] = cot_ref[:, m * n : (m + 1) * n].astype(F32).T
    count = 2 * half
    place = lax.broadcasted_iota(jnp.int32, (count, count), 0)
    lane = lax.broadcasted_iota(jnp.int32, (count, count), 1)
    wanted = jnp.where(lane < half, 2 * lane, 2 * (lane - half) + 1)
    pick = (place == wanted).astype(BF16)
    row = bases_ref[...].astype(F32).astype(BF16)
    split = dot(jnp.broadcast_to(row, (8, count)), pick, NN)
    hold[pl.ds(3, n, stride=LINE), :] = jnp.broadcast_to(split[0:1, :half], (n, half))
    hold[pl.ds(4, n, stride=LINE), :] = jnp.broadcast_to(split[0:1, half:], (n, half))
    weight = weight_ref[...].astype(F32)
    rows = []
    for m in range(cols):
        rows += [weight[:, m * n : (m + 1) * n], jnp.zeros((ROWS - share, n), F32)]
    rows.append(jnp.zeros((half - cols * ROWS, n), F32))
    hold[pl.ds(5, n, stride=LINE), :] = jnp.concatenate(rows, axis=0).T
    out_ref[...] = hold[...].astype(BF16)


def main_kernel(
    layers, seq, win, me_ref, got_ref, stem_ref, gain_ref, parts_ref, gained_ref, gram_ref, chosen_ref, turn_ref, out_ref, hold, symbols
):
    n = seq * win
    plane = n // layers
    channels = stem_ref.shape[1]
    cols = channels // n
    hold[: LINE * n, :] = got_ref[...].astype(F32)
    hold[LINE * n :, :] = jnp.zeros((8, 128), F32)
    chosen = chosen_ref[...]
    turn = turn_ref[...]

    own = hold[pl.ds(5, n, stride=LINE), :].T[: ROWS * cols].astype(BF16)
    share, block = KW * channels // n, min(256, channels)
    spread = []
    for at in range(0, KW * channels, block):
        low, high = at // share // 128 * 128, ((at + block - 1) // share // 128 + 1) * 128
        spread.append(dot(own[:, low:high], chosen[low:high, at : at + block], NN))
    spread = jnp.concatenate(spread, axis=1)
    line = [
        jnp.sum(spread[ROWS * m : ROWS * (m + 1)] * turn, axis=0, keepdims=True)
        for m in range(cols)
    ]
    line = jnp.concatenate(line + [jnp.zeros_like(line[0])] * (4 - cols), axis=0)
    weights = jnp.concatenate(
        [line[:, t * channels : (t + 1) * channels] for t in range(KW)], axis=0
    ).astype(BF16)
    mixed = dot(weights, gained_ref[...], NT)
    mixed = mixed[:, 0:TAPS] + mixed[:, 24 : 24 + TAPS] + mixed[:, 48 : 48 + TAPS]
    blank = jnp.zeros((4, 4), F32)
    table = []
    for t in range(KW):
        tap = mixed[4 * t : 4 * t + 4]
        pair = [jnp.concatenate([tap, blank], axis=1), jnp.concatenate([blank, tap], axis=1)]
        table += pair if t % 2 == 0 else pair[::-1]
    table = [part.astype(F32) for part in pieces(jnp.concatenate(table, axis=0), 3)]
    table = jnp.concatenate([jnp.concatenate(table, axis=1), gram_ref[...]], axis=0).astype(BF16)

    width = 128 * CELLS
    count = seq // CELLS
    sub = lax.broadcasted_iota(jnp.int32, (8, 128), 0)
    lane = lax.broadcasted_iota(jnp.int32, (8, 128), 1)
    wide = lax.broadcasted_iota(jnp.int32, (8, width), 0)
    top = wide < 4
    first, last = lane == 0, lane == 127
    base = (wide % 4).astype(F32)
    early, low = wide % 2 == 0, wide % 4 < 2

    def swap(x):
        return pltpu.roll(x, 4, 0)

    def quad_sum(x):
        x = x + jnp.where(early, pltpu.roll(x, 7, 0), pltpu.roll(x, 1, 0))
        return x + jnp.where(low, pltpu.roll(x, 6, 0), pltpu.roll(x, 2, 0))

    def turn_cells(x, by):
        return [pltpu.roll(x[:, 128 * i : 128 * i + 128], by, 1) for i in range(CELLS)]

    def down(prior, turned):
        shifted = [0.0 if prior is None else prior[-1]] + turned[:-1]
        return jnp.concatenate([jnp.where(first, a, b) for a, b in zip(shifted, turned)], axis=1)

    def up(later, turned):
        shifted = turned[1:] + [0.0 if later is None else later[0]]
        return jnp.concatenate([jnp.where(last, a, b) for a, b in zip(shifted, turned)], axis=1)

    side = lax.broadcasted_iota(jnp.int32, (win, 128), 1)
    for parity in range(2):
        own = hold[pl.ds(3 + parity, n, stride=LINE), :]
        own = [own[win * s : win * s + win] for s in range(seq)]
        behind = [-1.0] + [pltpu.roll(x, 1, 1) for x in own]
        ahead = [pltpu.roll(x, 127, 1) for x in own] + [-1.0]
        for s in range(seq):
            symbols[parity, pl.ds(win * s, win), :] = jnp.where(side == 0, behind[s], behind[s + 1])
            symbols[2 + parity, pl.ds(win * s, win), :] = own[s]
            symbols[4 + parity, pl.ds(win * s, win), :] = jnp.where(side == 127, ahead[s + 1], ahead[s])

    def load(w, c):
        dr, hots = [], [[], [], []]
        for s in range(c * CELLS, (c + 1) * CELLS):
            at = s * win + w
            cell = jnp.where(sub < cols, hold[LINE * at : LINE * at + 8, :], 0.0)
            dr.append(cell + pltpu.roll(cell, 4, 0))
            for i in range(3):
                pair = [
                    jnp.broadcast_to(symbols[2 * i + parity, pl.ds(at, 1), :], (8, 128))
                    for parity in range(2)
                ]
                hots[i].append(jnp.where(sub < 4, *pair))
        hots = [jnp.maximum(1.0 - jnp.abs(jnp.concatenate(x, axis=1) - base), 0.0) for x in hots]
        return jnp.concatenate(dr, axis=1), jnp.concatenate(hots, axis=0)

    def look(cell):
        dr, hots = cell
        narrow = hots.astype(BF16)
        looked = dot(table, jnp.concatenate([narrow] * 3, axis=0), NN)
        taps = [looked[8 * t : 8 * t + 8] for t in range(KW)]
        mean_e = looked[40:48] * hots[0:8] + looked[48:56] * hots[8:16]
        mean_o = looked[56:64] * hots[8:16] + looked[64:72] * hots[16:24]
        mean = jnp.where(top, mean_e, mean_o) + swap(jnp.where(top, mean_o, mean_e))
        scale = lax.rsqrt(jnp.maximum(quad_sum(mean), 0.0) + 1e-06)
        swapped = swap(scale)
        p0, p2, p4 = taps[0] * scale, taps[2] * scale, taps[4] * scale
        p1, p3 = taps[1] * swapped, taps[3] * swapped
        behind = turn_cells(p0 + jnp.where(top, p1, 0.0), 1)
        ahead = turn_cells(p4 + jnp.where(top, 0.0, p3), 127)
        return (p2 + jnp.where(top, p3, p1), ahead, behind), (
            hots, narrow, taps, scale, swapped, dr
        )

    def slope(prior, cell, later, dr):
        pre = cell[0] + down(prior and prior[2], cell[2]) + up(later and later[1], cell[1])
        dpre = dr * twice_gelu_slope(pre)
        return dpre, turn_cells(dpre, 127), turn_cells(dpre, 1)

    def close(prior, cell, later, kept):
        hots, narrow, taps, scale, swapped, dr = kept
        dpre = cell[0]
        ahead = up(later and later[1], cell[1])
        behind = down(prior and prior[2], cell[2])
        d1 = jnp.where(top, ahead, dpre)
        d3 = jnp.where(top, dpre, behind)
        here = taps[0] * ahead + taps[2] * dpre + taps[4] * behind
        there = taps[1] * d1 + taps[3] * d3
        bend = here + swap(there)
        bend = pltpu.roll(bend, 1, 0) + pltpu.roll(bend, 2, 0) + pltpu.roll(bend, 3, 0)
        bend = bend * (scale * scale * scale)
        rows = [ahead * scale, d1 * swapped, dpre * scale, d3 * swapped, behind * scale, dr]
        even = jnp.broadcast_to(bend[3:4], bend.shape)
        odd = jnp.broadcast_to(bend[7:8], bend.shape)
        rows += [even * hots[0:8], even * hots[8:16], odd * hots[8:16], odd * hots[16:24]]
        return dot(jnp.concatenate(rows, axis=0), hots, NT)

    total = jnp.zeros((80, 24), F32)
    jobs = []
    for w in range(win):
        jobs += [(w, c) for c in range(count)]
    looked, kept, slopes = {}, {}, {}
    for step in range(len(jobs) + LAG + LAG):
        if step < len(jobs):
            job = jobs[step]
            looked[job], kept[job] = look(load(*job))
        if 0 <= step - LAG < len(jobs):
            w, c = jobs[step - LAG]
            slopes[w, c] = slope(
                looked.get((w, c - 1)), looked[w, c], looked.get((w, c + 1)), kept[w, c][5]
            )
        if 0 <= step - LAG - LAG < len(jobs):
            w, c = jobs[step - LAG - LAG]
            total = total + close(
                slopes.get((w, c - 1)), slopes[w, c], slopes.get((w, c + 1)), kept[w, c]
            )

    stem = stem_ref[...]
    gain = gain_ref[...]
    total = 0.25 * total
    sums = []
    for t in range(KW + 1):
        cell = total[8 * t : 8 * t + 8]
        even, odd = (cell[0:4], cell[4:8]) if t % 2 == 0 or t == KW else (cell[4:8], cell[0:4])
        sums.append(even[:, :TAPS] + odd[:, 4:])
    grads = jnp.concatenate(sums[:KW], axis=0)
    even, odd = total[48:64, :TAPS], total[64:80, 4:]
    same = lax.broadcasted_iota(jnp.int32, (4, 4), 0) == lax.broadcasted_iota(jnp.int32, (4, 4), 1)
    even_end = [even[:, 16:].T, jnp.where(same, jnp.sum(even[12:16, 16:], axis=0, keepdims=True), 0.0)]
    odd_end = [jnp.where(same, jnp.sum(odd[0:4, :4], axis=0, keepdims=True), 0.0), odd[:, :4].T]
    crossed = jnp.concatenate([even, jnp.concatenate(even_end, axis=1)], axis=0)
    crossed = crossed + jnp.concatenate([jnp.concatenate(odd_end, axis=1), odd], axis=0)
    conv = split_dot(grads, gained_ref)
    conv = jnp.concatenate([conv[4 * t : 4 * t + 4] for t in range(KW)], axis=1)
    conv = jnp.concatenate([conv[m : m + 1] * turn for m in range(cols)], axis=0)
    conv = jnp.concatenate(pieces(conv, 2), axis=0)
    turned = [jnp.zeros((min(16, n), 2 * ROWS * cols), F32)] * max(1, n // 16)
    for at in range(0, KW * channels, block):
        low, high = at // share // 16, (at + block - 1) // share // 16 + 1
        part = dot(chosen[16 * low : 16 * high, at : at + block], conv[:, at : at + block], NT)
        for i in range(low, high):
            turned[i] = turned[i] + part[16 * (i - low) : 16 * (i - low + 1)]
    turned = jnp.concatenate(turned, axis=0)
    turned = turned[:, : ROWS * cols] + turned[:, ROWS * cols :]
    back = jnp.zeros((TAPS, channels), F32)
    for part in pieces(grads.T, 3):
        back = back + dot(part, weights, NN)
    stem_part = gain * back - split_dot(crossed * (1.0 / channels), parts_ref)
    gain_part = jnp.sum(stem * back, axis=0, keepdims=True)
    small = jnp.concatenate([stem_part, gain_part], axis=0)
    direct = jnp.concatenate([2.0 * sums[KW].T, jnp.zeros((1, 4), F32)], axis=0)
    mine = lax.broadcasted_iota(jnp.int32, (SUMS, n), 1) == me_ref[0]
    rows = []
    for m in range(cols):
        rows.append(small[:, m * n : (m + 1) * n] + jnp.where(mine, direct[:, m : m + 1], 0.0))
    rows.append(jnp.zeros((128 - cols * (ROWS + SUMS), n), F32))
    rows = jnp.concatenate([turned, jnp.concatenate(rows, axis=0).T], axis=1)
    for layer in range(layers):
        out_ref[pl.ds(layer, plane, stride=layers), :] = rows[layer * plane : (layer + 1) * plane]


def relay_kernel(layers, got_ref, out_ref):
    plane = got_ref.shape[0] // layers
    half = plane // 2
    total = got_ref[0:layers, :]
    for source in range(1, plane):
        total = total + got_ref[source * layers : (source + 1) * layers, :]
    total = [pltpu.roll(total, 48, 1), pltpu.roll(total, 16, 1)]
    total += [jnp.zeros((half - 2 * layers, 128), F32)] if half > 2 * layers else []
    total = jnp.concatenate(total, axis=0)
    lane = lax.broadcasted_iota(jnp.int32, total.shape, 1)
    for layer in range(layers):
        rows = got_ref[pl.ds(layer, plane, stride=layers), :]
        pair = jnp.where(lane < 48, rows[:half], pltpu.roll(rows[half:], 48, 1))
        out_ref[layer * half : (layer + 1) * half, :] = jnp.where(lane < 96, pair, total)


def total_kernel(layers, plane, got_ref, out_ref):
    half = plane // 2
    parts = []
    for at in (0, layers):
        part = got_ref[at : at + layers, :]
        for layer in range(1, layers):
            part = part + got_ref[layer * half + at : layer * half + at + layers, :]
        parts.append(part)
    lane = lax.broadcasted_iota(jnp.int32, parts[0].shape, 1)
    total = jnp.where(lane < 32, pltpu.roll(parts[0], 32, 1), pltpu.roll(parts[1], 64, 1))
    for target in range(plane):
        out_ref[target * layers : (target + 1) * layers, :] = total


def finish_kernel(layers, conv_ref, small_ref, grad_ref, stem_ref, gain_ref):
    n = small_ref.shape[0]
    plane, share = n // layers, grad_ref.shape[0]
    half = plane // 2
    cols = stem_ref.shape[1] // n
    conv = []
    for layer in range(layers):
        cell = conv_ref[layer * half : (layer + 1) * half, :]
        conv += [cell, pltpu.roll(cell, 128 - 48, 1)]
    conv = jnp.concatenate(conv, axis=0).T
    small = [small_ref[pl.ds(layer, plane, stride=layers), :] for layer in range(layers)]
    small = jnp.concatenate(small, axis=0).T
    for m in range(cols):
        lanes = slice(m * n, (m + 1) * n)
        grad_ref[:, lanes] = conv[ROWS * m : ROWS * m + share]
        stem_ref[:, lanes] = small[SUMS * m : SUMS * m + TAPS]
        gain_ref[lanes] = small[SUMS * m + TAPS]


def call(kernel, name, out, operands, scratch=(), smem=0, space=pltpu.VMEM, limit=48):
    specs = [pl.BlockSpec(memory_space=pltpu.SMEM)] * smem
    specs += [pl.BlockSpec(memory_space=space)] * (len(operands) - smem)
    many = isinstance(out, tuple)
    spec = pl.BlockSpec(memory_space=pltpu.VMEM)
    return pl.pallas_call(
        kernel,
        name=name,
        out_shape=out,
        in_specs=specs,
        out_specs=(spec,) * len(out) if many else spec,
        scratch_shapes=list(scratch),
        compiler_params=pltpu.CompilerParams(vmem_limit_bytes=limit * 1024 * 1024),
    )(*operands)


def exchange(x, axes):
    return lax.all_to_all(x, axes, 0, 0, tiled=True)


def shards(bases, stem_weight, norm_gain, conv_weight, cotangent):
    layers, win = lax.axis_size("layer"), lax.axis_size("win")
    seq = layers * lax.axis_size("row")
    n = seq * win
    plane = n // layers
    channels = norm_gain.shape[0]
    cols = channels // n
    half = bases.shape[1] // 2
    share = conv_weight.shape[0]
    me = lax.axis_index(AXES)

    sent = call(
        functools.partial(pack_kernel, n),
        "pack",
        jax.ShapeDtypeStruct((LINE * n, half), BF16),
        (bases, conv_weight, cotangent[0]),
        [
            pltpu.VMEM(bases.shape, jnp.int32),
            pltpu.VMEM(conv_weight.shape, BF16),
            pltpu.VMEM(cotangent.shape[1:], BF16),
            pltpu.VMEM((LINE * n, half), F32),
            pltpu.SemaphoreType.DMA((3,)),
        ],
        space=pltpu.HBM,
        limit=60,
    )
    got = exchange(sent.reshape(n, LINE // 2, 2, half), AXES).reshape(LINE * n, half)

    parts, gained = [
        jnp.concatenate([jnp.pad(part, ((0, 4), (0, 0))) for part in outer_pieces(x, 3)], axis=0)
        for x in (stem_weight, stem_weight * norm_gain)
    ]
    gram = jnp.dot(stem_weight, stem_weight.T, precision=HIGH) * (1.0 / channels)
    tap = jnp.arange(TAPS) // 4
    ahead, same = tap[None] > tap[:, None], tap[None] == tap[:, None]
    square = jnp.diag(gram)[None]
    even = gram * (2.0 * ahead + same) + square * ((tap[:, None] == 3) & (tap[None] == 4))
    odd = gram * (2.0 * ahead.T + same) + square * ((tap[:, None] == 1) & (tap[None] == 0))
    even, odd = jnp.pad(even[:16], ((0, 0), (0, 4))), jnp.pad(odd[4:], ((0, 0), (4, 0)))
    gram = jnp.concatenate([even, odd], axis=0)
    gram = jnp.concatenate([part.astype(F32) for part in outer_pieces(gram, 3)], axis=1)
    row = jnp.arange(KW * channels, dtype=jnp.int32)[None, :]
    chosen = (row // share == jnp.arange(n, dtype=jnp.int32)[:, None]).astype(BF16)
    turn = (row % share == jnp.arange(ROWS, dtype=jnp.int32)[:, None]).astype(F32)

    packed = call(
        functools.partial(main_kernel, layers, seq, win),
        "main",
        jax.ShapeDtypeStruct((n, 128), F32),
        (me.reshape(1), got, stem_weight, norm_gain[None], parts, gained, gram, chosen, turn),
        [pltpu.VMEM((LINE * n + 8, 128), F32), pltpu.VMEM((6, n, 128), F32)],
        1,
    )
    got = exchange(packed.reshape(plane, layers, 128), PLANE).reshape(n, 128)
    relayed = call(
        functools.partial(relay_kernel, layers),
        "relay",
        jax.ShapeDtypeStruct((n // 2, 128), F32),
        (got,),
    )
    conv = exchange(relayed.reshape(layers, plane // 2, 128), "layer").reshape(n // 2, 128)
    total = call(
        functools.partial(total_kernel, layers, plane),
        "total",
        jax.ShapeDtypeStruct((n, 128), F32),
        (conv,),
    )
    small = exchange(total.reshape(plane, layers, 128), PLANE).reshape(n, 128)
    return call(
        functools.partial(finish_kernel, layers),
        "finish",
        (
            jax.ShapeDtypeStruct((share, channels), F32),
            jax.ShapeDtypeStruct((TAPS, channels), F32),
            jax.ShapeDtypeStruct((channels,), F32),
        ),
        (conv, small),
    )


def solution(mesh):
    seq, win = mesh.devices.shape
    layers = LAYERS if seq % LAYERS == 0 else 1
    mesh = Mesh(mesh.devices.reshape(layers, seq // layers, win), AXES)
    line = ("layer", "row")
    in_specs = (P("win", line), P(), P(), P(AXES, None), P("win", line, None))
    out_specs = (P(AXES, None), P(), P())
    return jax.shard_map(shards, mesh=mesh, in_specs=in_specs, out_specs=out_specs, check_vma=False)
```

```python
import functools

import jax
import jax.numpy as jnp
from jax import lax
from jax.experimental import pallas as pl
from jax.experimental.pallas import tpu as pltpu
from jax.sharding import Mesh, PartitionSpec as P

KW = 5
TAPS = 4 * KW
PLANE = ("row", "win")
AXES = ("layer",) + PLANE
F32 = jnp.float32
BF16 = jnp.bfloat16
HIGH = lax.Precision.HIGHEST
ROOT = 0.7978845608028654
CUBE = 0.044715
ROWS, SUMS, LINE = 16, TAPS + 1, 6
CELLS = 2
PARTS = 2
LAG = 1
LAYERS = 8
NN, NT = (((1,), (0,)), ((), ())), (((1,), (1,)), ((), ()))


def pieces(x, count):
    out = []
    for _ in range(count):
        top = x.astype(BF16)
        out.append(top)
        x = x - top.astype(F32)
    return out


def outer_pieces(x, count):
    out = []
    for _ in range(count):
        top = lax.reduce_precision(x, 8, 7)
        out.append(top.astype(BF16))
        x = x - top
    return out


def dot(a, b, dims, precision=None):
    return lax.dot_general(a, b, dims, precision=precision, preferred_element_type=F32)


def split_dot(a, b_ref):
    blank = jnp.zeros((a.shape[0], 4), F32)
    big, small = [jnp.concatenate([x.astype(F32), blank], axis=1) for x in pieces(a, 2)]
    left = jnp.concatenate([big, big, big, small, small], axis=1).astype(BF16)
    return dot(left, jnp.concatenate([b_ref[...], b_ref[:48]], axis=0), NN)


def twice_gelu_slope(x):
    sq = x * x
    th = jnp.tanh(x * (ROOT + (ROOT * CUBE) * sq))
    return (1.0 + th) * (1.0 + (1.0 - th) * (x * (ROOT + (3.0 * ROOT * CUBE) * sq)))


def pack_kernel(
    n, bases_hbm, weight_hbm, cot_hbm, out_hbm, bases_ref, weight_ref, cot_ref, hold, out_ref, sems
):
    pairs = ((bases_hbm, bases_ref), (weight_hbm, weight_ref), (cot_hbm, cot_ref))
    copies = [pltpu.make_async_copy(*pair, sems.at[i]) for i, pair in enumerate(pairs)]
    for copy in copies:
        copy.start()
    half = cot_ref.shape[0]
    share, channels = weight_ref.shape
    cols = channels // n
    count = 2 * half
    place = lax.broadcasted_iota(jnp.int32, (count, count), 0)
    lane = lax.broadcasted_iota(jnp.int32, (count, count), 1)
    wanted = jnp.where(lane < half, 2 * lane, 2 * (lane - half) + 1)
    pick = (place == wanted).astype(BF16)
    copies[0].wait()
    row = bases_ref[...].astype(F32).astype(BF16)
    split = dot(jnp.broadcast_to(row, (8, count)), pick, NN)
    hold[pl.ds(3, n, stride=LINE), :] = jnp.broadcast_to(split[0:1, :half], (n, half))
    hold[pl.ds(4, n, stride=LINE), :] = jnp.broadcast_to(split[0:1, half:], (n, half))
    copies[1].wait()
    weight = weight_ref[...].astype(F32)
    rows = []
    for m in range(cols):
        rows += [weight[:, m * n : (m + 1) * n], jnp.zeros((ROWS - share, n), F32)]
    rows.append(jnp.zeros((half - cols * ROWS, n), F32))
    hold[pl.ds(5, n, stride=LINE), :] = jnp.concatenate(rows, axis=0).T
    copies[2].wait()
    part = n // PARTS
    for i in range(PARTS):
        for m in range(cols):
            at = m * n + i * part
            cell = cot_ref[:, at : at + part].astype(F32).T
            hold[pl.ds(LINE * part * i + m, part, stride=LINE), :] = cell
        lines = slice(LINE * part * i, LINE * part * (i + 1))
        out_ref[lines, :] = hold[lines, :].astype(BF16)
        copies.append(pltpu.make_async_copy(out_ref.at[lines], out_hbm.at[lines], sems.at[3 + i]))
        copies[-1].start()
    for copy in copies[3:]:
        copy.wait()


def main_kernel(
    layers, seq, win, me_ref, got_ref, stem_ref, gain_ref, parts_ref, gained_ref, gram_ref, chosen_ref, turn_ref, out_ref, hold, symbols
):
    n = seq * win
    plane = n // layers
    channels = stem_ref.shape[1]
    cols = channels // n
    hold[: LINE * n, :] = got_ref[...].astype(F32)
    hold[LINE * n :, :] = jnp.zeros((8, 128), F32)
    chosen = chosen_ref[...]
    turn = turn_ref[...]

    own = hold[pl.ds(5, n, stride=LINE), :].T[: ROWS * cols].astype(BF16)
    share, block = KW * channels // n, min(256, channels)
    spread = []
    for at in range(0, KW * channels, block):
        low, high = at // share // 128 * 128, ((at + block - 1) // share // 128 + 1) * 128
        spread.append(dot(own[:, low:high], chosen[low:high, at : at + block], NN))
    spread = jnp.concatenate(spread, axis=1)
    line = [
        jnp.sum(spread[ROWS * m : ROWS * (m + 1)] * turn, axis=0, keepdims=True)
        for m in range(cols)
    ]
    line = jnp.concatenate(line + [jnp.zeros_like(line[0])] * (4 - cols), axis=0)
    weights = jnp.concatenate(
        [line[:, t * channels : (t + 1) * channels] for t in range(KW)], axis=0
    ).astype(BF16)
    mixed = dot(weights, gained_ref[...], NT)
    mixed = mixed[:, 0:TAPS] + mixed[:, 24 : 24 + TAPS] + mixed[:, 48 : 48 + TAPS]
    blank = jnp.zeros((4, 4), F32)
    table = []
    for t in range(KW):
        tap = mixed[4 * t : 4 * t + 4]
        pair = [jnp.concatenate([tap, blank], axis=1), jnp.concatenate([blank, tap], axis=1)]
        table += pair if t % 2 == 0 else pair[::-1]
    table = [part.astype(F32) for part in pieces(jnp.concatenate(table, axis=0), 3)]
    table = jnp.concatenate([jnp.concatenate(table, axis=1), gram_ref[...]], axis=0).astype(BF16)

    width = 128 * CELLS
    count = seq // CELLS
    sub = lax.broadcasted_iota(jnp.int32, (8, 128), 0)
    lane = lax.broadcasted_iota(jnp.int32, (8, 128), 1)
    wide = lax.broadcasted_iota(jnp.int32, (8, width), 0)
    top = wide < 4
    first, last = lane == 0, lane == 127
    base = (wide % 4).astype(F32)
    early, low = wide % 2 == 0, wide % 4 < 2

    def swap(x):
        return pltpu.roll(x, 4, 0)

    def quad_sum(x):
        x = x + jnp.where(early, pltpu.roll(x, 7, 0), pltpu.roll(x, 1, 0))
        return x + jnp.where(low, pltpu.roll(x, 6, 0), pltpu.roll(x, 2, 0))

    def turn_cells(x, by):
        return [pltpu.roll(x[:, 128 * i : 128 * i + 128], by, 1) for i in range(CELLS)]

    def down(prior, turned):
        shifted = [0.0 if prior is None else prior[-1]] + turned[:-1]
        return jnp.concatenate([jnp.where(first, a, b) for a, b in zip(shifted, turned)], axis=1)

    def up(later, turned):
        shifted = turned[1:] + [0.0 if later is None else later[0]]
        return jnp.concatenate([jnp.where(last, a, b) for a, b in zip(shifted, turned)], axis=1)

    side = lax.broadcasted_iota(jnp.int32, (win, 128), 1)
    for parity in range(2):
        own = hold[pl.ds(3 + parity, n, stride=LINE), :]
        own = [own[win * s : win * s + win] for s in range(seq)]
        behind = [-1.0] + [pltpu.roll(x, 1, 1) for x in own]
        ahead = [pltpu.roll(x, 127, 1) for x in own] + [-1.0]
        for s in range(seq):
            symbols[parity, pl.ds(win * s, win), :] = jnp.where(side == 0, behind[s], behind[s + 1])
            symbols[2 + parity, pl.ds(win * s, win), :] = own[s]
            symbols[4 + parity, pl.ds(win * s, win), :] = jnp.where(side == 127, ahead[s + 1], ahead[s])

    def load(w, c):
        dr, hots = [], [[], [], []]
        for s in range(c * CELLS, (c + 1) * CELLS):
            at = s * win + w
            cell = jnp.where(sub < cols, hold[LINE * at : LINE * at + 8, :], 0.0)
            dr.append(cell + pltpu.roll(cell, 4, 0))
            for i in range(3):
                pair = [
                    jnp.broadcast_to(symbols[2 * i + parity, pl.ds(at, 1), :], (8, 128))
                    for parity in range(2)
                ]
                hots[i].append(jnp.where(sub < 4, *pair))
        hots = [jnp.concatenate(x, axis=1) - base for x in hots]
        hots = jnp.maximum(1.0 - jnp.abs(jnp.concatenate(hots, axis=0).astype(BF16)), 0.0)
        return jnp.concatenate(dr, axis=1), hots

    def look(cell):
        dr, narrow = cell
        hots = narrow.astype(F32)
        looked = dot(table, jnp.concatenate([narrow] * 3, axis=0), NN)
        taps = [looked[8 * t : 8 * t + 8] for t in range(KW)]
        mean_e = looked[40:48] * hots[0:8] + looked[48:56] * hots[8:16]
        mean_o = looked[56:64] * hots[8:16] + looked[64:72] * hots[16:24]
        mean = jnp.where(top, mean_e, mean_o) + swap(jnp.where(top, mean_o, mean_e))
        scale = lax.rsqrt(jnp.maximum(quad_sum(mean), 0.0) + 1e-06)
        swapped = swap(scale)
        p0, p2, p4 = taps[0] * scale, taps[2] * scale, taps[4] * scale
        p1, p3 = taps[1] * swapped, taps[3] * swapped
        behind = turn_cells(p0 + jnp.where(top, p1, 0.0), 1)
        ahead = turn_cells(p4 + jnp.where(top, 0.0, p3), 127)
        return (p2 + jnp.where(top, p3, p1), ahead, behind), (
            hots, narrow, taps, scale, swapped, dr
        )

    def slope(prior, cell, later, dr):
        pre = cell[0] + down(prior and prior[2], cell[2]) + up(later and later[1], cell[1])
        dpre = dr * twice_gelu_slope(pre)
        return dpre, turn_cells(dpre, 127), turn_cells(dpre, 1)

    def close(prior, cell, later, kept):
        hots, narrow, taps, scale, swapped, dr = kept
        dpre = cell[0]
        ahead = up(later and later[1], cell[1])
        behind = down(prior and prior[2], cell[2])
        d1 = jnp.where(top, ahead, dpre)
        d3 = jnp.where(top, dpre, behind)
        here = taps[0] * ahead + taps[2] * dpre + taps[4] * behind
        there = taps[1] * d1 + taps[3] * d3
        bend = here + swap(there)
        bend = pltpu.roll(bend, 1, 0) + pltpu.roll(bend, 2, 0) + pltpu.roll(bend, 3, 0)
        bend = bend * (scale * scale * scale)
        rows = [ahead * scale, d1 * swapped, dpre * scale, d3 * swapped, behind * scale, dr]
        even = jnp.broadcast_to(bend[3:4], bend.shape)
        odd = jnp.broadcast_to(bend[7:8], bend.shape)
        rows += [even * hots[0:8], even * hots[8:16], odd * hots[8:16], odd * hots[16:24]]
        return dot(jnp.concatenate(rows, axis=0), hots, NT)

    total = jnp.zeros((80, 24), F32)
    jobs = []
    for w in range(win):
        jobs += [(w, c) for c in range(count)]
    looked, kept, slopes = {}, {}, {}
    for step in range(len(jobs) + LAG + LAG):
        if step < len(jobs):
            job = jobs[step]
            looked[job], kept[job] = look(load(*job))
        if 0 <= step - LAG < len(jobs):
            w, c = jobs[step - LAG]
            slopes[w, c] = slope(
                looked.get((w, c - 1)), looked[w, c], looked.get((w, c + 1)), kept[w, c][5]
            )
        if 0 <= step - LAG - LAG < len(jobs):
            w, c = jobs[step - LAG - LAG]
            total = total + close(
                slopes.get((w, c - 1)), slopes[w, c], slopes.get((w, c + 1)), kept[w, c]
            )

    stem = stem_ref[...]
    gain = gain_ref[...]
    total = 0.25 * total
    sums = []
    for t in range(KW + 1):
        cell = total[8 * t : 8 * t + 8]
        even, odd = (cell[0:4], cell[4:8]) if t % 2 == 0 or t == KW else (cell[4:8], cell[0:4])
        sums.append(even[:, :TAPS] + odd[:, 4:])
    grads = jnp.concatenate(sums[:KW], axis=0)
    even, odd = total[48:64, :TAPS], total[64:80, 4:]
    same = lax.broadcasted_iota(jnp.int32, (4, 4), 0) == lax.broadcasted_iota(jnp.int32, (4, 4), 1)
    even_end = [even[:, 16:].T, jnp.where(same, jnp.sum(even[12:16, 16:], axis=0, keepdims=True), 0.0)]
    odd_end = [jnp.where(same, jnp.sum(odd[0:4, :4], axis=0, keepdims=True), 0.0), odd[:, :4].T]
    crossed = jnp.concatenate([even, jnp.concatenate(even_end, axis=1)], axis=0)
    crossed = crossed + jnp.concatenate([jnp.concatenate(odd_end, axis=1), odd], axis=0)
    conv = split_dot(grads, gained_ref)
    conv = jnp.concatenate([conv[4 * t : 4 * t + 4] for t in range(KW)], axis=1)
    conv = jnp.concatenate([conv[m : m + 1] * turn for m in range(cols)], axis=0)
    conv = jnp.concatenate(pieces(conv, 2), axis=0)
    turned = [jnp.zeros((min(16, n), 2 * ROWS * cols), F32)] * max(1, n // 16)
    for at in range(0, KW * channels, block):
        low, high = at // share // 16, (at + block - 1) // share // 16 + 1
        part = dot(chosen[16 * low : 16 * high, at : at + block], conv[:, at : at + block], NT)
        for i in range(low, high):
            turned[i] = turned[i] + part[16 * (i - low) : 16 * (i - low + 1)]
    turned = jnp.concatenate(turned, axis=0)
    turned = turned[:, : ROWS * cols] + turned[:, ROWS * cols :]
    back = jnp.zeros((TAPS, channels), F32)
    for part in pieces(grads.T, 3):
        back = back + dot(part, weights, NN)
    stem_part = gain * back - split_dot(crossed * (1.0 / channels), parts_ref)
    gain_part = jnp.sum(stem * back, axis=0, keepdims=True)
    small = jnp.concatenate([stem_part, gain_part], axis=0)
    direct = jnp.concatenate([2.0 * sums[KW].T, jnp.zeros((1, 4), F32)], axis=0)
    mine = lax.broadcasted_iota(jnp.int32, (SUMS, n), 1) == me_ref[0]
    rows = []
    for m in range(cols):
        rows.append(small[:, m * n : (m + 1) * n] + jnp.where(mine, direct[:, m : m + 1], 0.0))
    rows.append(jnp.zeros((128 - cols * (ROWS + SUMS), n), F32))
    rows = jnp.concatenate([turned, jnp.concatenate(rows, axis=0).T], axis=1)
    for layer in range(layers):
        out_ref[pl.ds(layer, plane, stride=layers), :] = rows[layer * plane : (layer + 1) * plane]


def relay_kernel(layers, got_ref, out_ref):
    plane = got_ref.shape[0] // layers
    half = plane // 2
    total = got_ref[0:layers, :]
    for source in range(1, plane):
        total = total + got_ref[source * layers : (source + 1) * layers, :]
    total = [pltpu.roll(total, 48, 1), pltpu.roll(total, 16, 1)]
    total += [jnp.zeros((half - 2 * layers, 128), F32)] if half > 2 * layers else []
    total = jnp.concatenate(total, axis=0)
    lane = lax.broadcasted_iota(jnp.int32, total.shape, 1)
    for layer in range(layers):
        rows = got_ref[pl.ds(layer, plane, stride=layers), :]
        pair = jnp.where(lane < 48, rows[:half], pltpu.roll(rows[half:], 48, 1))
        out_ref[layer * half : (layer + 1) * half, :] = jnp.where(lane < 96, pair, total)


def total_kernel(layers, plane, got_ref, out_ref):
    half = plane // 2
    parts = []
    for at in (0, layers):
        part = got_ref[at : at + layers, :]
        for layer in range(1, layers):
            part = part + got_ref[layer * half + at : layer * half + at + layers, :]
        parts.append(part)
    lane = lax.broadcasted_iota(jnp.int32, parts[0].shape, 1)
    total = jnp.where(lane < 32, pltpu.roll(parts[0], 32, 1), pltpu.roll(parts[1], 64, 1))
    for target in range(plane):
        out_ref[target * layers : (target + 1) * layers, :] = total


def finish_kernel(layers, conv_ref, small_ref, grad_ref, stem_ref, gain_ref):
    n = small_ref.shape[0]
    plane, share = n // layers, grad_ref.shape[0]
    half = plane // 2
    cols = stem_ref.shape[1] // n
    conv = []
    for layer in range(layers):
        cell = conv_ref[layer * half : (layer + 1) * half, :]
        conv += [cell, pltpu.roll(cell, 128 - 48, 1)]
    conv = jnp.concatenate(conv, axis=0).T
    small = [small_ref[pl.ds(layer, plane, stride=layers), :] for layer in range(layers)]
    small = jnp.concatenate(small, axis=0).T
    for m in range(cols):
        lanes = slice(m * n, (m + 1) * n)
        grad_ref[:, lanes] = conv[ROWS * m : ROWS * m + share]
        stem_ref[:, lanes] = small[SUMS * m : SUMS * m + TAPS]
        gain_ref[lanes] = small[SUMS * m + TAPS]


def call(kernel, name, out, operands, scratch=(), smem=0, space=pltpu.VMEM, out_space=pltpu.VMEM, limit=48):
    specs = [pl.BlockSpec(memory_space=pltpu.SMEM)] * smem
    specs += [pl.BlockSpec(memory_space=space)] * (len(operands) - smem)
    many = isinstance(out, tuple)
    spec = pl.BlockSpec(memory_space=out_space)
    return pl.pallas_call(
        kernel,
        name=name,
        out_shape=out,
        in_specs=specs,
        out_specs=(spec,) * len(out) if many else spec,
        scratch_shapes=list(scratch),
        compiler_params=pltpu.CompilerParams(vmem_limit_bytes=limit * 1024 * 1024),
    )(*operands)


def exchange(x, axes):
    return lax.all_to_all(x, axes, 0, 0, tiled=True)


def shards(bases, stem_weight, norm_gain, conv_weight, cotangent):
    layers, win = lax.axis_size("layer"), lax.axis_size("win")
    seq = layers * lax.axis_size("row")
    n = seq * win
    plane = n // layers
    channels = norm_gain.shape[0]
    cols = channels // n
    half = bases.shape[1] // 2
    share = conv_weight.shape[0]
    me = lax.axis_index(AXES)

    sent = call(
        functools.partial(pack_kernel, n),
        "pack",
        jax.ShapeDtypeStruct((LINE * n, half), BF16),
        (bases, conv_weight, cotangent[0]),
        [
            pltpu.VMEM(bases.shape, jnp.int32),
            pltpu.VMEM(conv_weight.shape, BF16),
            pltpu.VMEM(cotangent.shape[1:], BF16),
            pltpu.VMEM((LINE * n, half), F32),
            pltpu.VMEM((LINE * n, half), BF16),
            pltpu.SemaphoreType.DMA((3 + PARTS,)),
        ],
        space=pltpu.HBM,
        out_space=pltpu.HBM,
        limit=60,
    )
    got = exchange(sent.reshape(n, LINE // 2, 2, half), AXES).reshape(LINE * n, half)

    parts, gained = [
        jnp.concatenate([jnp.pad(part, ((0, 4), (0, 0))) for part in outer_pieces(x, 3)], axis=0)
        for x in (stem_weight, stem_weight * norm_gain)
    ]
    gram = jnp.dot(stem_weight, stem_weight.T, precision=HIGH) * (1.0 / channels)
    tap = jnp.arange(TAPS) // 4
    ahead, same = tap[None] > tap[:, None], tap[None] == tap[:, None]
    square = jnp.diag(gram)[None]
    even = gram * (2.0 * ahead + same) + square * ((tap[:, None] == 3) & (tap[None] == 4))
    odd = gram * (2.0 * ahead.T + same) + square * ((tap[:, None] == 1) & (tap[None] == 0))
    even, odd = jnp.pad(even[:16], ((0, 0), (0, 4))), jnp.pad(odd[4:], ((0, 0), (4, 0)))
    gram = jnp.concatenate([even, odd], axis=0)
    gram = jnp.concatenate([part.astype(F32) for part in outer_pieces(gram, 3)], axis=1)
    row = jnp.arange(KW * channels, dtype=jnp.int32)[None, :]
    chosen = (row // share == jnp.arange(n, dtype=jnp.int32)[:, None]).astype(BF16)
    turn = (row % share == jnp.arange(ROWS, dtype=jnp.int32)[:, None]).astype(F32)

    packed = call(
        functools.partial(main_kernel, layers, seq, win),
        "main",
        jax.ShapeDtypeStruct((n, 128), F32),
        (me.reshape(1), got, stem_weight, norm_gain[None], parts, gained, gram, chosen, turn),
        [pltpu.VMEM((LINE * n + 8, 128), F32), pltpu.VMEM((6, n, 128), F32)],
        1,
    )
    got = exchange(packed.reshape(plane, layers, 128), PLANE).reshape(n, 128)
    relayed = call(
        functools.partial(relay_kernel, layers),
        "relay",
        jax.ShapeDtypeStruct((n // 2, 128), F32),
        (got,),
    )
    conv = exchange(relayed.reshape(layers, plane // 2, 128), "layer").reshape(n // 2, 128)
    total = call(
        functools.partial(total_kernel, layers, plane),
        "total",
        jax.ShapeDtypeStruct((n, 128), F32),
        (conv,),
    )
    small = exchange(total.reshape(plane, layers, 128), PLANE).reshape(n, 128)
    return call(
        functools.partial(finish_kernel, layers),
        "finish",
        (
            jax.ShapeDtypeStruct((share, channels), F32),
            jax.ShapeDtypeStruct((TAPS, channels), F32),
            jax.ShapeDtypeStruct((channels,), F32),
        ),
        (conv, small),
    )


def solution(mesh):
    seq, win = mesh.devices.shape
    layers = LAYERS if seq % LAYERS == 0 else 1
    mesh = Mesh(mesh.devices.reshape(layers, seq // layers, win), AXES)
    line = ("layer", "row")
    in_specs = (P("win", line), P(), P(), P(AXES, None), P("win", line, None))
    out_specs = (P(AXES, None), P(), P())
    return jax.shard_map(shards, mesh=mesh, in_specs=in_specs, out_specs=out_specs, check_vma=False)
```
